32 devices in a mesh: dp: 8 (over z, y), expert: 4 (over x, core).
Axes of the slice: x: 2, y: 2, z: 4, core: 2. Of those that a mesh axis runs over, the one named last changes fastest.
Arguments:
- tokens: bfloat16 [4096, 2048], P(('dp', 'expert')), may hold values from -6 to 6
- choice_rows: int32 [8, 4, 128], P('dp', 'expert'), may hold values from 0 to 511, as said below
- gate_weights: float32 [8, 4, 128], P('dp', 'expert'), may hold values from 0.1 to 1
- w_gate: bfloat16 [4, 2048, 1024], P('expert', 'dp'), may hold values from -0.125 to 0.125
- w_up: bfloat16 [4, 2048, 1024], P('expert', 'dp'), may hold values from -0.125 to 0.125
- w_down: bfloat16 [4, 1024, 2048], P('expert', 'dp'), may hold values from -0.1875 to 0.1875
Outputs:
- mixed: bfloat16 [4096, 2048], P(('dp', 'expert'))
The draws below stay inside these ranges and needn't reach their ends.
Inputs may be any that keep to these rules, and one draw needn't show every extreme that they name: `choice_rows`: for each group and expert the 128 numbers are distinct; at most 64 of them lie among the 128 tokens of one device of the group (numbers k * 128 to (k + 1) * 128 - 1 belong to device k of the expert axis), and for every expert and group some device gives exactly 64.
All inputs are finite; a program needn't handle non-finite values.
Results may differ from the reference program's by a relative error of at most 0.0057.
Values may be sent and summed in bfloat16 or wider, within the bound.
No kernel may reach another device: no remote copies, remote signals or barrier semaphores. Data moves between devices by JAX's collectives and lax.ppermute only.
A program may use at most 64 MiB of HBM per device.

```python
import jax
import jax.numpy as jnp
from jax import lax

D = 2048
H = 1024
TOK_DEV = 128
EXPERTS = 4
GROUPS = 8
GROUP = 512
CAP = 128
TOKENS = 4096


def one_expert_rows(key):
    average = TOK_DEV // 4
    parts = jax.random.split(key, 5)
    amounts = jax.random.randint(parts[0], (EXPERTS,), 0, average + 1)
    anchor = jax.random.randint(parts[1], (), 0, EXPERTS)
    offset = jax.random.randint(parts[2], (), 1, EXPERTS)
    amounts = amounts.at[anchor].set(average)
    amounts = amounts.at[(anchor + offset) % EXPERTS].set(0)
    counts = average + amounts - jnp.roll(amounts, -offset)
    orders = jax.vmap(lambda inner: jax.random.permutation(inner, TOK_DEV))(jax.random.split(parts[3], EXPERTS))
    usable = jnp.arange(TOK_DEV)[None, :] < counts[:, None]
    numbers = jnp.arange(EXPERTS)[:, None] * TOK_DEV + orders
    shuffle = jax.random.permutation(parts[4], EXPERTS * TOK_DEV).reshape(EXPERTS, TOK_DEV)
    scores = jnp.where(usable, shuffle, shuffle + EXPERTS * TOK_DEV)
    ranking = jnp.argsort(scores.reshape(-1), stable=True)
    return numbers.reshape(-1)[ranking[:CAP]].astype(jnp.int32)


def draw_choice_rows(key, part):
    keys = jax.random.split(key, GROUPS * EXPERTS)
    picks = jax.vmap(one_expert_rows)(keys)
    return picks.reshape(GROUPS, EXPERTS, CAP)


def steps_of(own_key, dims, cuts, smallest, largest):
    gain, own = 1.0, jax.random.fold_in(own_key, 6)
    for position, blocks in cuts:
        steps = jnp.exp(jax.random.uniform(jax.random.fold_in(own, position), (blocks,), jnp.float32, smallest / len(cuts), largest / len(cuts)))
        gain = gain * jnp.repeat(steps, dims[position] // blocks).reshape([-1 if axis == position else 1 for axis in range(len(dims))])
    return gain


def normal_values(own_key, extent, width, most, pieces=(), dtype=jnp.bfloat16):
    values = jax.random.normal(own_key, extent, jnp.float32) * width
    if len(pieces) > 0:
        values = steps_of(own_key, extent, pieces, -0.22, 0.18) * values
    return jnp.clip(values, min=-most, max=most).astype(dtype)


def setup_inputs(seed: int = 0) -> dict:
    seeds = jax.random.split(jax.random.key(seed), 7)
    return {
        "tokens": normal_values(seeds[0], (TOKENS, D), 1.0, 6.0, ((0, 32),)),
        "choice_rows": draw_choice_rows(jax.random.fold_in(seeds[6], 71), 0),
        "gate_weights": jnp.clip(0.1 + 0.9 * jax.random.uniform(seeds[2], (GROUPS, EXPERTS, CAP), jnp.float32) ** steps_of(seeds[2], (GROUPS, EXPERTS, CAP), ((0, 8), (1, 4)), -0.2, 0.2), 0.1, 1.0),
        "w_gate": normal_values(seeds[3], (EXPERTS, D, H), D ** -0.5, 0.125, ((0, 4), (1, 8))),
        "w_up": normal_values(seeds[4], (EXPERTS, D, H), D ** -0.5, 0.125, ((0, 4), (1, 8))),
        "w_down": normal_values(seeds[5], (EXPERTS, H, D), H ** -0.5, 0.1875, ((0, 4), (1, 8))),
    }


def reference(tokens, choice_rows, gate_weights, w_gate, w_up, w_down):
    grouped = tokens.reshape(GROUPS, GROUP, D)
    gate_full = w_gate.astype(jnp.float32)
    up_full = w_up.astype(jnp.float32)
    down_full = w_down.astype(jnp.float32)

    def one_group(packed):
        group_rows, picks, weights = packed
        picked = group_rows[picks.astype(jnp.int32)].astype(jnp.float32)
        gate = jnp.einsum("ecd,edh->ech", picked, gate_full)
        up_val = jnp.einsum("ecd,edh->ech", picked, up_full)
        hidden = (jax.nn.silu(gate) * up_val).astype(jnp.bfloat16)
        expert_out = jnp.einsum("ech,ehd->ecd", hidden.astype(jnp.float32), down_full)
        contribution = (weights[:, :, None] * expert_out).astype(jnp.bfloat16)
        total = jnp.zeros((GROUP, D), jnp.float32)
        total = total.at[picks.reshape(-1).astype(jnp.int32)].add(contribution.reshape(-1, D).astype(jnp.float32))
        return total.astype(jnp.bfloat16)

    mixed = lax.map(one_group, (grouped, choice_rows, gate_weights))
    return mixed.reshape(TOKENS, D)
```

```python
import functools

import jax
import jax.numpy as jnp
from jax import lax
from jax.experimental import pallas as pl
from jax.experimental.pallas import tpu as pltpu
from jax.sharding import PartitionSpec as P

CHUNKS = 2
F32 = jnp.float32
BF16 = jnp.bfloat16


def swap(value, axis, mask):
    pairs = [(source, source ^ mask) for source in range(lax.axis_size(axis))]
    return lax.ppermute(value, axis, pairs)


def after(value, *others):
    return lax.optimization_barrier((value, *others))[0]


def call(kernel, out_shape, *args, flops=0, scalars=0):
    in_specs = [pl.BlockSpec(memory_space=pltpu.SMEM)] * scalars
    in_specs += [pl.BlockSpec(memory_space=pltpu.VMEM)] * (len(args) - scalars)
    outs = out_shape if isinstance(out_shape, (list, tuple)) else [out_shape]
    size = sum(a.size * a.dtype.itemsize for a in (*args, *outs))
    return pl.pallas_call(
        kernel,
        out_shape=out_shape,
        in_specs=in_specs,
        out_specs=jax.tree.map(lambda _: pl.BlockSpec(memory_space=pltpu.VMEM), out_shape),
        compiler_params=pltpu.CompilerParams(vmem_limit_bytes=40 * 2**20),
        cost_estimate=pl.CostEstimate(flops=flops, bytes_accessed=size, transcendentals=0),
    )(*args)


def shape(*dims, dtype=BF16):
    return jax.ShapeDtypeStruct(dims, dtype)


def dot(a, b):
    return jnp.dot(a, b, preferred_element_type=F32)


def split_units(quarter_ref, gate_ref, up_ref, *out_refs, replicas):
    quarter = quarter_ref[0]
    rows, units = gate_ref.shape[1:]
    block = units // replicas
    for part in range(4):
        pieces = [
            ref[0, :, (4 * j + part) * block : (4 * j + part + 1) * block]
            for ref in (gate_ref, up_ref)
            for j in range(replicas // 4)
        ]
        value = jnp.concatenate(pieces, axis=1)
        for low in range(4):

            @pl.when((quarter ^ low) == part)
            def _():
                out_refs[low][...] = value


def ranks_of(hits):
    c = hits.shape[1]
    before = lax.broadcasted_iota(jnp.int32, (c, c), 0) < lax.broadcasted_iota(jnp.int32, (c, c), 1)
    return dot(hits.astype(BF16), before.astype(BF16)).astype(jnp.int32)


def own_tables(expert_ref, rows_ref, pick_ref, place_ref, *, experts, tok_dev):
    rows = rows_ref[...]
    capacity = rows.shape[1]
    block = (rows // tok_dev) ^ expert_ref[0]
    local = rows % tok_dev
    bits = experts.bit_length() - 1
    seat = jnp.zeros_like(block)
    for bit in range(bits):
        seat = seat | (((block >> bit) & 1) << (bits - 1 - bit))
    place = seat * tok_dev + local
    count = experts * tok_dev
    pick_ref[...] = (lax.broadcasted_iota(jnp.int32, (count, capacity), 0) == place).astype(BF16)
    hot = lax.broadcasted_iota(jnp.int32, (experts, capacity), 0) == block
    rank = jnp.sum(jnp.where(hot, ranks_of(hot.astype(F32)), 0), axis=0, keepdims=True)
    most = tok_dev // 2
    position = block * most + rank
    place_ref[...] = (
        lax.broadcasted_iota(jnp.int32, (experts * most, capacity), 0) == position
    ).astype(BF16)


def back_table(expert_ref, rows_ref, select_ref, *, experts, tok_dev):
    rows = rows_ref[...]
    capacity = rows.shape[1]
    most = tok_dev // 2
    hits = (rows // tok_dev) == expert_ref[0]
    local = jnp.where(hits, rows % tok_dev, -1)
    rank = ranks_of(hits.astype(F32))
    bits = experts.bit_length() - 1
    for mask in range(experts):
        seat = int(f"{mask:0{bits}b}"[::-1], 2) if bits else 0
        token = lax.broadcasted_iota(jnp.int32, (tok_dev, capacity), 0) == local[seat : seat + 1]
        slot = lax.broadcasted_iota(jnp.int32, (most, capacity), 0) == rank[seat : seat + 1]
        table = lax.dot_general(
            token.astype(BF16), slot.astype(BF16), (((1,), (1,)), ((), ())), preferred_element_type=F32
        )
        select_ref[:, mask * most : (mask + 1) * most] = table.astype(BF16)


def pick_rows(pick_ref, *refs):
    out_ref = refs[-1]
    total, start = 0.0, 0
    for ref in refs[:-1]:
        rows = ref.shape[0]
        total = total + lax.dot_general(
            pick_ref[start : start + rows, :],
            ref[...],
            (((0,), (0,)), ((), ())),
            preferred_element_type=F32,
        )
        start += rows
    out_ref[...] = total.astype(BF16)


def hidden_units(where_ref, own_ref, other_ref, *refs, pieces, reorder):
    weights, (keep_ref, send_ref, total) = refs[:pieces], refs[pieces:]
    tall = own_ref.shape[0]
    for index in range(pieces):
        rows = weights[index].shape[0]
        columns = pl.ds(pl.multiple_of(where_ref[index] * rows, min(rows, 256)), rows)
        for side, ref in enumerate((own_ref, other_ref)):
            lines = pl.ds(side * tall, tall)
            product = dot(ref[:, columns], weights[index][...])
            if index == 0:
                total[lines, :] = product
            else:
                total[lines, :] += product
    half = total.shape[1] // 2
    block = half // reorder
    for side, out_ref in enumerate((keep_ref, send_ref)):
        lines = pl.ds(side * tall, tall)
        for j in range(reorder):
            if reorder == 1:
                first, second = pl.ds(0, half), pl.ds(half, half)
            else:
                at = (where_ref[0] // 4) ^ j
                first = pl.ds(pl.multiple_of(at * block, 128), block)
                second = pl.ds(pl.multiple_of(half + at * block, 128), block)
            gate, up = total[lines, first], total[lines, second]
            out_ref[:, j * block : (j + 1) * block] = (gate / (1.0 + jnp.exp(-gate)) * up).astype(BF16)


def down_units(keep_ref, came_ref, *refs, pieces):
    own, other, (out_ref, away_ref) = refs[:pieces], refs[pieces : 2 * pieces], refs[2 * pieces :]
    capacity = out_ref.shape[0]
    for side, target in enumerate((out_ref, away_ref)):
        lines = pl.ds(side * capacity, capacity)
        total = 0.0
        for hidden, parts in ((keep_ref, own), (came_ref, other)):
            start = 0
            for part in parts:
                rows = part.shape[0]
                total = total + dot(hidden[lines, start : start + rows], part[...])
                start += rows
        target[...] = total.astype(target.dtype)


def weigh(place_ref, weights_ref, out_ref, away_ref, *sent_refs):
    total = out_ref[...] + away_ref[...].astype(F32)
    contribution = (weights_ref[...] * total).astype(BF16)
    most = sent_refs[0].shape[0]
    for block, ref in enumerate(sent_refs):
        ref[...] = dot(place_ref[block * most : (block + 1) * most, :], contribution).astype(BF16)


def mix(select_ref, *refs):
    returned, out_ref = refs[:-1], refs[-1]
    most = returned[0].shape[0]
    total = 0.0
    for block, ref in enumerate(returned):
        total = total + dot(select_ref[:, block * most : (block + 1) * most], ref[...])
    out_ref[...] = total.astype(BF16)


def per_device(tokens, choice_rows, gate_weights, w_gate, w_up, w_down):
    experts = lax.axis_size("expert")
    replicas = lax.axis_size("dp")
    expert = lax.axis_index("expert").astype(jnp.int32)
    replica = lax.axis_index("dp").astype(jnp.int32)
    tok_dev, width = tokens.shape
    most = tok_dev // 2
    own_rows = choice_rows[0]
    capacity = own_rows.shape[1]
    rows_shard, units = w_gate.shape[1:]
    block = units // replicas

    outgoing = call(
        functools.partial(split_units, replicas=replicas),
        [shape(rows_shard, units // 2)] * 4,
        (replica % 4)[None],
        w_gate,
        w_up,
        scalars=1,
    )
    weights = [outgoing[0]] + [None] * (replicas - 1)
    for mask in range(replicas - 1, 0, -1):
        weights[mask] = swap(outgoing[mask % 4], "dp", mask)

    group, every = [tokens], own_rows
    bit = experts // 2
    while bit > 0:
        have = group[0] if len(group) == 1 else jnp.concatenate(group, axis=0)
        group.append(swap(have, "expert", bit))
        every = jnp.concatenate([every, swap(every, "expert", bit)], axis=0)
        bit //= 2
    pick_hot, place_hot = call(
        functools.partial(own_tables, experts=experts, tok_dev=tok_dev),
        [shape(experts * tok_dev, capacity), shape(experts * most, capacity)],
        expert[None],
        own_rows,
        scalars=1,
    )
    picked = call(
        pick_rows,
        shape(capacity, width),
        pick_hot,
        *group,
        flops=2 * experts * tok_dev * capacity * width,
    )

    pair = jnp.concatenate([picked, swap(picked, "dp", 2)], axis=0)
    other_pair = swap(pair, "dp", 1)
    order = replica ^ jnp.arange(replicas, dtype=jnp.int32)
    aligned = rows_shard % 128 == 0
    if not aligned:
        weights = [jnp.take(jnp.stack(weights), order, axis=0).reshape(-1, units // 2)]
        order = jnp.zeros((1,), jnp.int32)
    reorder = replicas // 4 if block % 128 == 0 else 1
    keep, send = pl.pallas_call(
        functools.partial(hidden_units, pieces=len(weights), reorder=reorder),
        out_shape=[shape(2 * capacity, units // 4)] * 2,
        in_specs=[pl.BlockSpec(memory_space=pltpu.SMEM)]
        + [pl.BlockSpec(memory_space=pltpu.VMEM)] * (2 + len(weights)),
        out_specs=[pl.BlockSpec(memory_space=pltpu.VMEM)] * 2,
        scratch_shapes=[pltpu.VMEM((4 * capacity, units // 2), F32)],
        compiler_params=pltpu.CompilerParams(vmem_limit_bytes=40 * 2**20),
        cost_estimate=pl.CostEstimate(
            flops=4 * capacity * width * units, bytes_accessed=2**23, transcendentals=0
        ),
    )(order, pair, other_pair, *weights)
    came = swap(send, "dp", 1)

    gate_column = gate_weights[0, 0][:, None]
    step = width // CHUNKS
    select = call(
        functools.partial(back_table, experts=experts, tok_dev=tok_dev),
        shape(tok_dev, experts * most),
        expert[None],
        every,
        scalars=1,
    )
    results = []
    for chunk in range(CHUNKS):
        own = [after(w_down[0, :, chunk * step : (chunk + 1) * step], weights[-1])]
        other = [swap(own[0], "dp", 1)]
        bit = 4
        while bit < replicas:
            have = own[0] if len(own) == 1 else jnp.concatenate(own, axis=0)
            own.append(swap(have, "dp", bit))
            other.append(swap(own[-1], "dp", 1))
            bit *= 2
        if block % 128 != 0:
            turn = (replica // 4) ^ jnp.arange(replicas // 4, dtype=jnp.int32)
            own, other = (
                [jnp.concatenate(x, axis=0).reshape(replicas // 4, block, step)[turn].reshape(-1, step)]
                for x in (own, other)
            )
        out, away = call(
            functools.partial(down_units, pieces=len(own)),
            [shape(capacity, step, dtype=F32), shape(capacity, step)],
            keep,
            came,
            *own,
            *other,
            flops=2 * capacity * units * step,
        )
        sent = call(
            weigh,
            [shape(most, step)] * experts,
            place_hot,
            gate_column,
            out,
            swap(away, "dp", 2),
            flops=2 * experts * most * capacity * step,
        )
        returned = [sent[0]] + [swap(sent[c], "expert", c) for c in range(1, experts)]
        results.append(
            call(
                mix,
                shape(tok_dev, step),
                select,
                *returned,
                flops=2 * experts * most * tok_dev * step,
            )
        )
    return jnp.concatenate(results, axis=1)


def solution(mesh):
    return jax.shard_map(
        per_device,
        mesh=mesh,
        in_specs=(
            P(("dp", "expert"), None),
            P("dp", "expert", None),
            P("dp", "expert", None),
            P("expert", "dp", None),
            P("expert", "dp", None),
            P("expert", "dp", None),
        ),
        out_specs=P(("dp", "expert"), None),
        check_vma=False,
    )
```

```python
import functools

import jax
import jax.numpy as jnp
from jax import lax
from jax.experimental import pallas as pl
from jax.experimental.pallas import tpu as pltpu
from jax.sharding import PartitionSpec as P

SHARES = (5, 3)
OPENING_LIMIT = 60 * 2**20
F32 = jnp.float32
BF16 = jnp.bfloat16


def swap(value, axis, mask):
    pairs = [(source, source ^ mask) for source in range(lax.axis_size(axis))]
    return lax.ppermute(value, axis, pairs)


def call(kernel, out_shape, *args, wait=(), flops=0, scalars=0):
    args = (*args[:scalars], *wait, *args[scalars:])
    in_specs = [pl.BlockSpec(memory_space=pltpu.SMEM)] * scalars
    in_specs += [pl.BlockSpec(memory_space=pl.ANY)] * len(wait)
    in_specs += [pl.BlockSpec(memory_space=pltpu.VMEM)] * (len(args) - scalars - len(wait))
    outs = out_shape if isinstance(out_shape, (list, tuple)) else [out_shape]
    size = sum(a.size * a.dtype.itemsize for a in (*args, *outs))

    def body(*refs):
        kernel(*refs[:scalars], *refs[scalars + len(wait) :])

    return pl.pallas_call(
        body,
        out_shape=out_shape,
        in_specs=in_specs,
        out_specs=jax.tree.map(lambda _: pl.BlockSpec(memory_space=pltpu.VMEM), out_shape),
        compiler_params=pltpu.CompilerParams(vmem_limit_bytes=4 * size + 2**23),
        cost_estimate=pl.CostEstimate(flops=flops, bytes_accessed=size, transcendentals=0),
    )(*args)


def shape(*dims, dtype=BF16):
    return jax.ShapeDtypeStruct(dims, dtype)


def dot(a, b):
    return jnp.dot(a, b, preferred_element_type=F32)


def opening(bit_ref, gate_ref, up_ref, same_ref, other_ref, sem):
    pairs = sem.shape[0] // 4
    wide = gate_ref.shape[2] // (2 * pairs)
    copies = []
    for flip, target in ((0, same_ref), (1, other_ref)):
        at = 0
        for ref in (gate_ref, up_ref):
            for j in range(pairs):
                start = pl.multiple_of((2 * j + (bit_ref[0] ^ flip)) * wide, 128)
                copies.append(
                    pltpu.make_async_copy(
                        ref.at[0, :, pl.ds(start, wide)], target.at[:, at : at + wide], sem.at[len(copies)]
                    )
                )
                at += wide
    for copy in copies:
        copy.start()
    for copy in copies:
        copy.wait()


def hand(in_ref, out_ref):
    out_ref[...] = in_ref[...]


def ranks_of(hits):
    c = hits.shape[1]
    before = lax.broadcasted_iota(jnp.int32, (c, c), 0) < lax.broadcasted_iota(jnp.int32, (c, c), 1)
    return dot(hits.astype(BF16), before.astype(BF16)).astype(jnp.int32)


def own_tables(expert_ref, rows_ref, pick_ref, place_ref, tag_ref, *, experts, tok_dev):
    rows = rows_ref[...]
    capacity = rows.shape[1]
    block = (rows // tok_dev) ^ expert_ref[0]
    local = rows % tok_dev
    bits = experts.bit_length() - 1
    seat = jnp.zeros_like(block)
    for bit in range(bits):
        seat = seat | (((block >> bit) & 1) << (bits - 1 - bit))
    place = seat * tok_dev + local
    count = experts * tok_dev
    pick_ref[...] = (lax.broadcasted_iota(jnp.int32, (count, capacity), 0) == place).astype(BF16)
    hot = lax.broadcasted_iota(jnp.int32, (experts, capacity), 0) == block
    rank = jnp.sum(jnp.where(hot, ranks_of(hot.astype(F32)), 0), axis=0, keepdims=True)
    most = tok_dev // 2
    position = block * most + rank
    here = lax.broadcasted_iota(jnp.int32, (experts * most, capacity), 0) == position
    place_ref[...] = here.astype(BF16)
    number = jnp.sum(jnp.where(here, local + 1, 0).astype(F32), axis=1, keepdims=True)
    tag_ref[...] = jnp.broadcast_to(number, tag_ref.shape).astype(BF16)


def pick_rows(pick_ref, *refs):
    out_ref = refs[-1]
    total, start = 0.0, 0
    for ref in refs[:-1]:
        rows = ref.shape[0]
        total = total + lax.dot_general(
            pick_ref[start : start + rows, :],
            ref[...],
            (((0,), (0,)), ((), ())),
            preferred_element_type=F32,
        )
        start += rows
    out_ref[...] = total.astype(BF16)


def cut(down_ref, out_ref, *, start):
    out_ref[...] = down_ref[0, :, start : start + out_ref.shape[1]]


def hidden_units(where_ref, own_ref, far_ref, *refs, pairs):
    *weights, out_ref, total = refs
    capacity = own_ref.shape[0]
    rows = weights[0].shape[0]
    for mask, block in enumerate(weights):
        columns = pl.ds(pl.multiple_of(where_ref[mask] * rows, min(rows, 256)), rows)
        for side, ref in enumerate((own_ref, far_ref)):
            lines = pl.ds(side * capacity, capacity)
            product = dot(ref[:, columns], block[...])
            if mask == 0:
                total[lines, :] = product
            else:
                total[lines, :] += product
    half = total.shape[1] // 2
    if pairs == 0:
        gate, up = total[:, :half], total[:, half:]
        out_ref[...] = (gate / (1.0 + jnp.exp(-gate)) * up).astype(BF16)
        return
    block = half // (2 * pairs)
    device = where_ref[0]
    for y in range(2):
        for j in range(pairs):
            at = (2 * ((device // 4) ^ j) + ((device % 2) ^ y)) * block
            first = pl.ds(pl.multiple_of(at, 128), block)
            second = pl.ds(pl.multiple_of(half + at, 128), block)
            gate, up = total[:, first], total[:, second]
            at = (y * pairs + j) * block
            out_ref[:, at : at + block] = (gate / (1.0 + jnp.exp(-gate)) * up).astype(BF16)


def down_units(hidden_ref, *refs, places):
    parts, (out_ref, away_ref) = refs[:-2], refs[-2:]
    capacity, step = out_ref.shape
    for side, target in enumerate((out_ref, away_ref)):
        lines = pl.ds(side * capacity, capacity)
        total, unit = 0.0, 0
        for part, at in zip(parts, places):
            rows = part.shape[0]
            total = total + dot(hidden_ref[lines, unit : unit + rows], part[:, at : at + step])
            unit += rows
        target[...] = total.astype(target.dtype)


def weigh(place_ref, tag_ref, weights_ref, out_ref, away_ref, *sent_refs):
    total = out_ref[...] + away_ref[...].astype(F32)
    contribution = (weights_ref[...] * total).astype(BF16)
    step = total.shape[1]
    most, wide = sent_refs[0].shape
    for block, ref in enumerate(sent_refs):
        lines = pl.ds(block * most, most)
        ref[:, :step] = dot(place_ref[lines, :], contribution).astype(BF16)
        if wide > step:
            ref[:, step:] = tag_ref[lines, :]


def mix(*refs, step):
    returned, (select_ref, out_ref) = refs[:-2], refs[-2:]
    most, tok_dev = returned[0].shape[0], out_ref.shape[0]
    total = 0.0
    for block, ref in enumerate(returned):
        number = ref[:, step : step + 1].astype(jnp.int32) - 1
        table = (lax.broadcasted_iota(jnp.int32, (most, tok_dev), 1) == number).astype(BF16)
        select_ref[block * most : (block + 1) * most, :] = table
        total = total + lax.dot_general(
            table, ref[:, :step], (((0,), (0,)), ((), ())), preferred_element_type=F32
        )
    out_ref[...] = total.astype(BF16)


def mix_more(select_ref, *refs, ready):
    done, returned, out_ref = refs[:ready], refs[ready:-1], refs[-1]
    most = returned[0].shape[0]
    start = 0
    for ref in done:
        out_ref[:, start : start + ref.shape[1]] = ref[...]
        start += ref.shape[1]
    total = 0.0
    for block, ref in enumerate(returned):
        total = total + lax.dot_general(
            select_ref[block * most : (block + 1) * most, :],
            ref[...],
            (((0,), (0,)), ((), ())),
            preferred_element_type=F32,
        )
    out_ref[:, start:] = total.astype(BF16)


def per_device(tokens, choice_rows, gate_weights, w_gate, w_up, w_down):
    experts = lax.axis_size("expert")
    replicas = lax.axis_size("dp")
    expert = lax.axis_index("expert").astype(jnp.int32)
    replica = lax.axis_index("dp").astype(jnp.int32)
    tok_dev, width = tokens.shape
    most = tok_dev // 2
    own_rows = choice_rows[0]
    capacity = own_rows.shape[1]
    rows_shard, units = w_gate.shape[1:]
    block = units // replicas

    limit = 16 * 2**20 if capacity <= 128 else 48 * 2**20
    starts = [sum(SHARES[:i]) * width // sum(SHARES) for i in range(len(SHARES) + 1)]
    steps = [end - start for start, end in zip(starts, starts[1:])]
    down_rows = w_down.shape[1]
    pairs = replicas // 4
    zbit = replica // 2 % 2
    whole_lanes = block % 128 == 0
    if whole_lanes:
        same_units, other_units = pl.pallas_call(
            opening,
            out_shape=[shape(rows_shard, units)] * 2,
            in_specs=[pl.BlockSpec(memory_space=pltpu.SMEM)] + [pl.BlockSpec(memory_space=pl.ANY)] * 2,
            out_specs=[pl.BlockSpec(memory_space=pltpu.VMEM)] * 2,
            scratch_shapes=[pltpu.SemaphoreType.DMA((4 * pairs,))],
            compiler_params=pltpu.CompilerParams(vmem_limit_bytes=OPENING_LIMIT),
            cost_estimate=pl.CostEstimate(flops=0, bytes_accessed=2**21, transcendentals=0),
        )(zbit[None], w_gate, w_up)
    else:
        same_units, other_units = (
            jnp.concatenate(
                [
                    lax.dynamic_index_in_dim(
                        w[0].reshape(rows_shard, pairs, 2, 2 * block), zbit ^ flip, axis=2, keepdims=False
                    ).reshape(rows_shard, units // 2)
                    for w in (w_gate, w_up)
                ],
                axis=1,
            )
            for flip in (0, 1)
        )
    far = [mask for mask in range(replicas - 2, 2, -2)]
    weights = {0: same_units}
    weights[1] = swap(same_units, "dp", 1)
    for mask in far[::2]:
        weights[mask] = swap(other_units, "dp", mask)

    group = [tokens]
    bit = experts // 2
    while bit > 0:
        if bit == 1:
            ready = group[-1]
        group += [swap(x, "expert", bit) for x in group]
        bit //= 2
    late_units = call(hand, shape(rows_shard, units), same_units, wait=[ready])
    for mask in far[1::2]:
        weights[mask] = swap(late_units, "dp", mask)
    pick_hot, place_hot, tags = call(
        functools.partial(own_tables, experts=experts, tok_dev=tok_dev),
        [shape(experts * tok_dev, capacity), shape(experts * most, capacity), shape(experts * most, 128)],
        expert[None],
        own_rows,
        scalars=1,
    )
    picked = call(
        pick_rows,
        shape(capacity, width),
        pick_hot,
        *group,
        flops=2 * experts * tok_dev * capacity * width,
    )
    picked_z = swap(picked, "dp", 2)
    weights[2] = swap(other_units, "dp", 2)
    down_y = swap(w_down[0], "dp", 1)
    for mask in [2, *far]:
        weights[mask + 1] = swap(weights[mask], "dp", 1)

    down = []
    for index in range(len(SHARES)):
        piece = call(
            functools.partial(cut, start=starts[index]),
            shape(down_rows, steps[index]),
            w_down,
            wait=[weights[far[min(index, len(far) - 1)]]],
        )
        own, bit = [piece], 4
        while bit < replicas:
            have = own[0] if len(own) == 1 else jnp.concatenate(own, axis=0)
            own.append(swap(have, "dp", bit))
            bit *= 2
        down.append(own[1:])

    arrays = [weights[mask] for mask in range(replicas)]
    order = replica ^ jnp.arange(replicas, dtype=jnp.int32)
    if rows_shard % 128 != 0:
        arrays = [jnp.take(jnp.stack(arrays), order, axis=0).reshape(-1, units)]
        order = jnp.zeros((1,), jnp.int32)
    hidden = pl.pallas_call(
        functools.partial(hidden_units, pairs=pairs if whole_lanes else 0),
        out_shape=shape(2 * capacity, units // 2),
        in_specs=[pl.BlockSpec(memory_space=pltpu.SMEM)]
        + [pl.BlockSpec(memory_space=pltpu.VMEM)] * (2 + len(arrays)),
        out_specs=pl.BlockSpec(memory_space=pltpu.VMEM),
        scratch_shapes=[pltpu.VMEM((2 * capacity, units), F32)],
        compiler_params=pltpu.CompilerParams(vmem_limit_bytes=limit),
        cost_estimate=pl.CostEstimate(
            flops=4 * capacity * width * units, bytes_accessed=2**23, transcendentals=0
        ),
    )(order, picked, picked_z, *arrays)
    if not whole_lanes:
        index = jnp.arange(2 * pairs, dtype=jnp.int32)
        turn = 2 * ((replica // 4) ^ (index % pairs)) + ((replica % 2) ^ (index // pairs))
        hidden = jnp.take(hidden.reshape(-1, 2 * pairs, block), turn, axis=1).reshape(hidden.shape)

    gate_column = gate_weights[0, 0][:, None]
    results = []
    for index, (start, step, far_rows) in enumerate(zip(starts, steps, down)):
        parts = [w_down[0], *far_rows, down_y, *[swap(x, "dp", 1) for x in far_rows]]
        out, away = call(
            functools.partial(down_units, places=[start if x.shape[1] == width else 0 for x in parts]),
            [shape(capacity, step, dtype=F32), shape(capacity, step)],
            hidden,
            *parts,
            flops=2 * capacity * units * step,
        )
        extra = 128 if index == 0 else 0
        sent = call(
            weigh,
            [shape(most, step + extra)] * experts,
            place_hot,
            tags,
            gate_column,
            out,
            swap(away, "dp", 2),
            flops=2 * experts * most * capacity * step,
        )
        returned = [sent[0]] + [swap(sent[c], "expert", c) for c in range(1, experts)]
        flops = 2 * experts * most * tok_dev * step
        if index == 0:
            select, result = call(
                functools.partial(mix, step=step),
                [shape(experts * most, tok_dev), shape(tok_dev, step)],
                *returned,
                flops=flops,
            )
            results.append(result)
        else:
            last = index == len(SHARES) - 1
            ready = results if last else []
            results.append(
                call(
                    functools.partial(mix_more, ready=len(ready)),
                    shape(tok_dev, width if last else step),
                    select,
                    *ready,
                    *returned,
                    flops=flops,
                )
            )
    return results[-1]


def solution(mesh):
    return jax.shard_map(
        per_device,
        mesh=mesh,
        in_specs=(
            P(("dp", "expert"), None),
            P("dp", "expert", None),
            P("dp", "expert", None),
            P("expert", "dp", None),
            P("expert", "dp", None),
            P("expert", "dp", None),
        ),
        out_specs=P(("dp", "expert"), None),
        check_vma=False,
    )
```

```python
import functools

import jax
import jax.numpy as jnp
from jax import lax
from jax.experimental import pallas as pl
from jax.experimental.pallas import tpu as pltpu
from jax.sharding import PartitionSpec as P

SHARES = (5, 3)
OPENING_LIMIT = 60 * 2**20
LONG = 10**12
F32 = jnp.float32
BF16 = jnp.bfloat16


def swap(value, axis, mask):
    pairs = [(source, source ^ mask) for source in range(lax.axis_size(axis))]
    return lax.ppermute(value, axis, pairs)


def call(kernel, out_shape, *args, wait=(), flops=0, scalars=0):
    args = (*args[:scalars], *wait, *args[scalars:])
    in_specs = [pl.BlockSpec(memory_space=pltpu.SMEM)] * scalars
    in_specs += [pl.BlockSpec(memory_space=pl.ANY)] * len(wait)
    in_specs += [pl.BlockSpec(memory_space=pltpu.VMEM)] * (len(args) - scalars - len(wait))
    outs = out_shape if isinstance(out_shape, (list, tuple)) else [out_shape]
    size = sum(a.size * a.dtype.itemsize for a in (*args, *outs))

    def body(*refs):
        kernel(*refs[:scalars], *refs[scalars + len(wait) :])

    return pl.pallas_call(
        body,
        out_shape=out_shape,
        in_specs=in_specs,
        out_specs=jax.tree.map(lambda _: pl.BlockSpec(memory_space=pltpu.VMEM), out_shape),
        compiler_params=pltpu.CompilerParams(vmem_limit_bytes=4 * size + 2**23),
        cost_estimate=pl.CostEstimate(flops=flops, bytes_accessed=size, transcendentals=0),
    )(*args)


def shape(*dims, dtype=BF16):
    return jax.ShapeDtypeStruct(dims, dtype)


def dot(a, b):
    return jnp.dot(a, b, preferred_element_type=F32)


def opening(bit_ref, gate_ref, up_ref, *refs, flip, pairs):
    *more, out_ref, sem = refs
    rows = gate_ref.shape[1]
    wide = gate_ref.shape[2] // (2 * pairs)
    copies = []

    def copy(source, target):
        copies.append(pltpu.make_async_copy(source, target, sem.at[len(copies)]))

    at = 0
    for ref in (gate_ref, up_ref):
        for j in range(pairs):
            start = pl.multiple_of((2 * j + (bit_ref[0] ^ flip)) * wide, 128)
            copy(ref.at[0, :, pl.ds(start, wide)], out_ref.at[:rows, at : at + wide])
            at += wide
    for down_ref in more:
        tall, half = down_ref.shape[1], out_ref.shape[1]
        for j in range(down_ref.shape[2] // half):
            copy(
                down_ref.at[0, :, j * half : (j + 1) * half],
                out_ref.at[rows + j * tall : rows + (j + 1) * tall],
            )
    for item in copies:
        item.start()
    for item in copies:
        item.wait()


def join(*refs):
    out_ref, start = refs[-1], 0
    for ref in refs[:-1]:
        out_ref[start : start + ref.shape[0]] = ref[...]
        start += ref.shape[0]


def hand(*refs):
    half = len(refs) // 2
    for ref, out_ref in zip(refs[:half], refs[half:]):
        out_ref[...] = ref[: out_ref.shape[0]]


def ranks_of(hits):
    c = hits.shape[1]
    before = lax.broadcasted_iota(jnp.int32, (c, c), 0) < lax.broadcasted_iota(jnp.int32, (c, c), 1)
    return dot(hits.astype(BF16), before.astype(BF16)).astype(jnp.int32)


def own_tables(expert_ref, rows_ref, pick_ref, place_ref, tag_ref, *, experts, tok_dev):
    rows = rows_ref[...]
    capacity = rows.shape[1]
    block = (rows // tok_dev) ^ expert_ref[0]
    local = rows % tok_dev
    place = block * tok_dev + local
    count = experts * tok_dev
    pick_ref[...] = (lax.broadcasted_iota(jnp.int32, (count, capacity), 0) == place).astype(BF16)
    hot = lax.broadcasted_iota(jnp.int32, (experts, capacity), 0) == block
    rank = jnp.sum(jnp.where(hot, ranks_of(hot.astype(F32)), 0), axis=0, keepdims=True)
    most = tok_dev // 2
    position = block * most + rank
    here = lax.broadcasted_iota(jnp.int32, (experts * most, capacity), 0) == position
    place_ref[...] = here.astype(BF16)
    number = jnp.sum(jnp.where(here, local + 1, 0).astype(F32), axis=1, keepdims=True)
    tag_ref[...] = jnp.broadcast_to(number, tag_ref.shape).astype(BF16)


def pick_rows(pick_ref, *refs):
    out_ref = refs[-1]
    total, start = 0.0, 0
    for ref in refs[:-1]:
        rows = ref.shape[0]
        total = total + lax.dot_general(
            pick_ref[start : start + rows, :],
            ref[...],
            (((0,), (0,)), ((), ())),
            preferred_element_type=F32,
        )
        start += rows
    out_ref[...] = total.astype(BF16)


def cut(down_ref, out_ref, *, start):
    out_ref[...] = down_ref[0, :, start : start + out_ref.shape[1]]


def products(total, where_ref, own_ref, far_ref, arrays, places, fresh):
    capacity = own_ref.shape[0]
    for array, first, count, mask in places:
        columns = pl.ds(pl.multiple_of(where_ref[mask] * count, min(count, 256)), count)
        block = arrays[array][first : first + count, :]
        for side, ref in enumerate((own_ref, far_ref)):
            lines = pl.ds(side * capacity, capacity)
            product = dot(ref[:, columns], block)
            if fresh:
                total[lines, :] = product
            else:
                total[lines, :] += product
        fresh = False


def first_units(where_ref, own_ref, far_ref, *refs, places):
    *arrays, total = refs
    products(total, where_ref, own_ref, far_ref, arrays, places, True)


def hidden_units(where_ref, own_ref, far_ref, start_ref, *refs, places, pairs):
    *arrays, out_ref, total = refs
    total[...] = start_ref[...]
    products(total, where_ref, own_ref, far_ref, arrays, places, False)
    half = total.shape[1] // 2
    if pairs == 0:
        gate, up = total[:, :half], total[:, half:]
        out_ref[...] = (gate / (1.0 + jnp.exp(-gate)) * up).astype(BF16)
        return
    block = half // (2 * pairs)
    device = where_ref[0]
    for y in range(2):
        for j in range(pairs):
            at = (2 * ((device // 4) ^ j) + ((device % 2) ^ y)) * block
            first = pl.ds(pl.multiple_of(at, 128), block)
            second = pl.ds(pl.multiple_of(half + at, 128), block)
            gate, up = total[:, first], total[:, second]
            at = (y * pairs + j) * block
            out_ref[:, at : at + block] = (gate / (1.0 + jnp.exp(-gate)) * up).astype(BF16)


def down_units(hidden_ref, *refs, places):
    arrays, (out_ref, away_ref) = refs[:-2], refs[-2:]
    capacity = out_ref.shape[0]
    total, unit = 0.0, 0
    for pieces in places:
        values = [arrays[a][r : r + n, c : c + w] for a, r, n, c, w in pieces]
        block = values[0] if len(values) == 1 else jnp.concatenate(values, axis=1)
        rows = block.shape[0]
        total = total + dot(hidden_ref[:, unit : unit + rows], block)
        unit += rows
    out_ref[...] = total[:capacity]
    away_ref[...] = total[capacity:].astype(BF16)


def weigh(place_ref, tag_ref, weights_ref, out_ref, away_ref, *sent_refs):
    total = out_ref[...] + away_ref[...].astype(F32)
    contribution = (weights_ref[...] * total).astype(BF16)
    step = total.shape[1]
    most, wide = sent_refs[0].shape
    for block, ref in enumerate(sent_refs):
        lines = pl.ds(block * most, most)
        ref[:, :step] = dot(place_ref[lines, :], contribution).astype(BF16)
        if wide > step:
            ref[:, step:] = tag_ref[lines, :]


def mix(*refs, step):
    returned, (select_ref, out_ref) = refs[:-2], refs[-2:]
    most, tok_dev = returned[0].shape[0], out_ref.shape[0]
    total = 0.0
    for block, ref in enumerate(returned):
        number = ref[:, step : step + 1].astype(jnp.int32) - 1
        table = (lax.broadcasted_iota(jnp.int32, (most, tok_dev), 1) == number).astype(BF16)
        select_ref[block * most : (block + 1) * most, :] = table
        total = total + lax.dot_general(
            table, ref[:, :step], (((0,), (0,)), ((), ())), preferred_element_type=F32
        )
    out_ref[...] = total.astype(BF16)


def mix_more(select_ref, *refs, ready):
    done, returned, out_ref = refs[:ready], refs[ready:-1], refs[-1]
    most = returned[0].shape[0]
    start = 0
    for ref in done:
        out_ref[:, start : start + ref.shape[1]] = ref[...]
        start += ref.shape[1]
    total = 0.0
    for block, ref in enumerate(returned):
        total = total + lax.dot_general(
            select_ref[block * most : (block + 1) * most, :],
            ref[...],
            (((0,), (0,)), ((), ())),
            preferred_element_type=F32,
        )
    out_ref[:, start:] = total.astype(BF16)


def per_device(tokens, choice_rows, gate_weights, w_gate, w_up, w_down):
    experts = lax.axis_size("expert")
    replicas = lax.axis_size("dp")
    expert = lax.axis_index("expert").astype(jnp.int32)
    replica = lax.axis_index("dp").astype(jnp.int32)
    tok_dev, width = tokens.shape
    most = tok_dev // 2
    own_rows = choice_rows[0]
    capacity = own_rows.shape[1]
    rows_shard, units = w_gate.shape[1:]
    block = units // replicas

    limit = 16 * 2**20 if capacity <= 128 else 48 * 2**20
    starts = [sum(SHARES[:i]) * width // sum(SHARES) for i in range(len(SHARES) + 1)]
    steps = [end - start for start, end in zip(starts, starts[1:])]
    down_rows = w_down.shape[1]
    pairs = replicas // 4
    zbit = replica // 2 % 2
    whole_lanes = block % 128 == 0
    if whole_lanes:
        def collect(flip, *arrays):
            count = sum(x.shape[1] * x.shape[2] for x in arrays[2:]) // units
            return pl.pallas_call(
                functools.partial(opening, flip=flip, pairs=pairs),
                out_shape=shape(rows_shard + count, units),
                in_specs=[pl.BlockSpec(memory_space=pltpu.SMEM)]
                + [pl.BlockSpec(memory_space=pl.ANY)] * len(arrays),
                out_specs=pl.BlockSpec(memory_space=pltpu.VMEM),
                scratch_shapes=[pltpu.SemaphoreType.DMA((2 * pairs + width // units,))],
                compiler_params=pltpu.CompilerParams(vmem_limit_bytes=OPENING_LIMIT),
                cost_estimate=pl.CostEstimate(flops=0, bytes_accessed=2**20, transcendentals=0),
            )(zbit[None], *arrays)

        other_units = collect(1, w_gate, w_up)
        across = collect(0, w_gate, w_up, w_down)
    else:
        same_units, other_units = (
            jnp.concatenate(
                [
                    lax.dynamic_index_in_dim(
                        w[0].reshape(rows_shard, pairs, 2, 2 * block), zbit ^ flip, axis=2, keepdims=False
                    ).reshape(rows_shard, units // 2)
                    for w in (w_gate, w_up)
                ],
                axis=1,
            )
            for flip in (0, 1)
        )
        halves = [w_down[0, :, at : at + units] for at in range(0, width, units)]
        across = jnp.concatenate([same_units, *halves], axis=0)
    far = [mask for mask in range(replicas - 2, 2, -2)]
    came = swap(across, "dp", 1)
    weights = {mask: swap(other_units, "dp", mask) for mask in far[::2]}

    weights[2] = swap(other_units, "dp", 2)

    def down_far(piece):
        own, bit = [piece], 4
        while bit < replicas:
            have = own[0] if len(own) == 1 else jnp.concatenate(own, axis=0)
            own.append(swap(have, "dp", bit))
            bit *= 2
        return own[1:]

    late_same = call(hand, [shape(rows_shard, units)], across)[0]
    for mask in far[1::2]:
        weights[mask] = swap(late_same, "dp", mask)

    group = [tokens]
    bit = 1
    while bit < experts:
        have = group[0]
        if len(group) > 1:
            have = call(join, shape(bit * tok_dev, width), *group, wait=[other_units])
        group.append(swap(have, "expert", bit))
        bit *= 2
    pick_hot, place_hot, tags = call(
        functools.partial(own_tables, experts=experts, tok_dev=tok_dev),
        [shape(experts * tok_dev, capacity), shape(experts * most, capacity), shape(experts * most, 128)],
        expert[None],
        own_rows,
        scalars=1,
    )
    picked = call(
        pick_rows,
        shape(capacity, width),
        pick_hot,
        *group,
        wait=[came],
        flops=LONG,
    )
    picked_z = swap(picked, "dp", 2)
    group_far = [2, *far[::2]]
    came_far = [swap(weights[mask], "dp", 1) for mask in group_far]
    for mask in far[1::2]:
        weights[mask + 1] = swap(weights[mask], "dp", 1)

    down, down_far_y = [], []
    for index in range(len(SHARES)):
        piece = call(
            functools.partial(cut, start=starts[index]),
            shape(down_rows, steps[index]),
            w_down,
            wait=[weights[far[0]]] if index == 0 else [weights[far[-1]]] if index == 1 else down[-1],
            flops=LONG if index == 0 else 0,
        )
        down.append(down_far(piece))
        down_far_y.append([swap(x, "dp", 1) for x in down[-1]])

    order = replica ^ jnp.arange(replicas, dtype=jnp.int32)
    late = [mask for mask in range(2, replicas) if mask & ~1 in far[1::2]]
    arrays = [across, came, *came_far, *[weights[mask] for mask in group_far]]
    places = [(0, 0, rows_shard, 0), (1, 0, rows_shard, 1)]
    for i, mask in enumerate(group_far):
        places += [(2 + len(group_far) + i, 0, rows_shard, mask), (2 + i, 0, rows_shard, mask + 1)]
    late_arrays = [weights[mask] for mask in late]
    late_places = [(i, 0, rows_shard, mask) for i, mask in enumerate(late)]
    if rows_shard % 128 != 0:
        blocks = {m: arrays[a][r : r + n] for a, r, n, m in places}
        blocks |= {m: late_arrays[a][r : r + n] for a, r, n, m in late_places}
        stacked = jnp.take(jnp.stack([blocks[m] for m in range(replicas)]), order, axis=0).reshape(-1, units)
        parts = stacked.shape[0] // 2
        arrays, late_arrays = [stacked[:parts]], [stacked[parts:]]
        places, late_places = [(0, 0, parts, 0)], [(0, 0, parts, 1)]
        order = jnp.arange(2, dtype=jnp.int32)
    flops = capacity * width * units
    start_units = call(
        functools.partial(first_units, places=places),
        shape(2 * capacity, units, dtype=F32),
        order,
        picked,
        picked_z,
        *arrays,
        flops=3 * flops,
        scalars=1,
    )
    hidden = pl.pallas_call(
        functools.partial(hidden_units, places=late_places, pairs=pairs if whole_lanes else 0),
        out_shape=shape(2 * capacity, units // 2),
        in_specs=[pl.BlockSpec(memory_space=pltpu.SMEM)]
        + [pl.BlockSpec(memory_space=pltpu.VMEM)] * (3 + len(late_arrays)),
        out_specs=pl.BlockSpec(memory_space=pltpu.VMEM),
        scratch_shapes=[pltpu.VMEM((2 * capacity, units), F32)],
        compiler_params=pltpu.CompilerParams(vmem_limit_bytes=limit),
        cost_estimate=pl.CostEstimate(flops=flops, bytes_accessed=2**22, transcendentals=0),
    )(order, picked, picked_z, start_units, *late_arrays)
    if not whole_lanes:
        index = jnp.arange(2 * pairs, dtype=jnp.int32)
        turn = 2 * ((replica // 4) ^ (index % pairs)) + ((replica % 2) ^ (index // pairs))
        hidden = jnp.take(hidden.reshape(-1, 2 * pairs, block), turn, axis=1).reshape(hidden.shape)

    gate_column = gate_weights[0, 0][:, None]
    results = []
    for index, (start, step, far_rows) in enumerate(zip(starts, steps, down)):
        def pieces(array, first, at, end):
            cuts = [(at, min(end, units)), (max(at, units), end)]
            return [
                (array, first + down_rows * (c // units), down_rows, c % units, e - c) for c, e in cuts if c < e
            ]

        parts = [across, came, *far_rows, *down_far_y[index]]
        count = len(far_rows)
        places = [pieces(0, rows_shard, start, start + step)]
        places += [[(2 + i, 0, x.shape[0], 0, step)] for i, x in enumerate(far_rows)]
        places += [pieces(1, rows_shard, start, start + step)]
        places += [[(2 + count + i, 0, x.shape[0], 0, step)] for i, x in enumerate(far_rows)]
        out, away = call(
            functools.partial(down_units, places=places),
            [shape(capacity, step, dtype=F32), shape(capacity, step)],
            hidden,
            *parts,
            flops=2 * capacity * units * step,
        )
        extra = 128 if index == 0 else 0
        sent = call(
            weigh,
            [shape(most, step + extra)] * experts,
            place_hot,
            tags,
            gate_column,
            out,
            swap(away, "dp", 2),
            flops=2 * experts * most * capacity * step,
        )
        returned = [sent[0]] + [swap(sent[c], "expert", c) for c in range(1, experts)]
        flops = 2 * experts * most * tok_dev * step
        if index == 0:
            select, result = call(
                functools.partial(mix, step=step),
                [shape(experts * most, tok_dev), shape(tok_dev, step)],
                *returned,
                flops=flops,
            )
            results.append(result)
        else:
            last = index == len(SHARES) - 1
            ready = results if last else []
            results.append(
                call(
                    functools.partial(mix_more, ready=len(ready)),
                    shape(tok_dev, width if last else step),
                    select,
                    *ready,
                    *returned,
                    flops=flops,
                )
            )
    return results[-1]


def solution(mesh):
    return jax.shard_map(
        per_device,
        mesh=mesh,
        in_specs=(
            P(("dp", "expert"), None),
            P("dp", "expert", None),
            P("dp", "expert", None),
            P("expert", "dp", None),
            P("expert", "dp", None),
            P("expert", "dp", None),
        ),
        out_specs=P(("dp", "expert"), None),
        check_vma=False,
    )
```

```python
import functools

import jax
import jax.numpy as jnp
from jax import lax
from jax.experimental import pallas as pl
from jax.experimental.pallas import tpu as pltpu
from jax.sharding import PartitionSpec as P

SHARES = (9, 7)
OPENING_LIMIT = 60 * 2**20
LONG = 10**12
F32 = jnp.float32
BF16 = jnp.bfloat16


def swap(value, axis, mask):
    pairs = [(source, source ^ mask) for source in range(lax.axis_size(axis))]
    return lax.ppermute(value, axis, pairs)


def call(kernel, out_shape, *args, wait=(), flops=0, scalars=0):
    args = (*args[:scalars], *wait, *args[scalars:])
    in_specs = [pl.BlockSpec(memory_space=pltpu.SMEM)] * scalars
    in_specs += [pl.BlockSpec(memory_space=pl.ANY)] * len(wait)
    in_specs += [pl.BlockSpec(memory_space=pltpu.VMEM)] * (len(args) - scalars - len(wait))
    outs = out_shape if isinstance(out_shape, (list, tuple)) else [out_shape]
    size = sum(a.size * a.dtype.itemsize for a in (*args, *outs))

    def body(*refs):
        kernel(*refs[:scalars], *refs[scalars + len(wait) :])

    return pl.pallas_call(
        body,
        out_shape=out_shape,
        in_specs=in_specs,
        out_specs=jax.tree.map(lambda _: pl.BlockSpec(memory_space=pltpu.VMEM), out_shape),
        compiler_params=pltpu.CompilerParams(vmem_limit_bytes=4 * size + 2**23),
        cost_estimate=pl.CostEstimate(flops=flops, bytes_accessed=size, transcendentals=0),
    )(*args)


def shape(*dims, dtype=BF16):
    return jax.ShapeDtypeStruct(dims, dtype)


def dot(a, b):
    return jnp.dot(a, b, preferred_element_type=F32)


def opening(bit_ref, gate_ref, up_ref, *refs, flip, pairs):
    *more, out_ref, sem = refs
    rows = gate_ref.shape[1]
    wide = gate_ref.shape[2] // (2 * pairs)
    copies = []

    def copy(source, target):
        copies.append(pltpu.make_async_copy(source, target, sem.at[len(copies)]))

    at = 0
    for ref in (gate_ref, up_ref):
        for j in range(pairs):
            start = pl.multiple_of((2 * j + (bit_ref[0] ^ flip)) * wide, 128)
            copy(ref.at[0, :, pl.ds(start, wide)], out_ref.at[:rows, at : at + wide])
            at += wide
    for down_ref in more:
        tall, half = down_ref.shape[1], out_ref.shape[1]
        for j in range(down_ref.shape[2] // half):
            copy(
                down_ref.at[0, :, j * half : (j + 1) * half],
                out_ref.at[rows + j * tall : rows + (j + 1) * tall],
            )
    for item in copies:
        item.start()
    for item in copies:
        item.wait()


def join(*refs):
    out_ref, start = refs[-1], 0
    for ref in refs[:-1]:
        out_ref[start : start + ref.shape[0]] = ref[...]
        start += ref.shape[0]


def hand(*refs):
    half = len(refs) // 2
    for ref, out_ref in zip(refs[:half], refs[half:]):
        out_ref[...] = ref[: out_ref.shape[0]]


def ranks_of(hits):
    c = hits.shape[1]
    before = lax.broadcasted_iota(jnp.int32, (c, c), 0) < lax.broadcasted_iota(jnp.int32, (c, c), 1)
    return dot(hits.astype(BF16), before.astype(BF16)).astype(jnp.int32)


def own_tables(expert_ref, rows_ref, pick_ref, place_ref, tag_ref, *, experts, tok_dev):
    rows = rows_ref[...]
    capacity = rows.shape[1]
    block = (rows // tok_dev) ^ expert_ref[0]
    local = rows % tok_dev
    place = block * tok_dev + local
    count = experts * tok_dev
    pick_ref[...] = (lax.broadcasted_iota(jnp.int32, (count, capacity), 0) == place).astype(BF16)
    hot = lax.broadcasted_iota(jnp.int32, (experts, capacity), 0) == block
    rank = jnp.sum(jnp.where(hot, ranks_of(hot.astype(F32)), 0), axis=0, keepdims=True)
    most = tok_dev // 2
    position = block * most + rank
    here = lax.broadcasted_iota(jnp.int32, (experts * most, capacity), 0) == position
    place_ref[...] = here.astype(BF16)
    number = jnp.sum(jnp.where(here, local + 1, 0).astype(F32), axis=1, keepdims=True)
    tag_ref[...] = jnp.broadcast_to(number, tag_ref.shape).astype(BF16)


def pick_rows(pick_ref, *refs):
    out_ref = refs[-1]
    total, start = 0.0, 0
    for ref in refs[:-1]:
        rows = ref.shape[0]
        total = total + lax.dot_general(
            pick_ref[start : start + rows, :],
            ref[...],
            (((0,), (0,)), ((), ())),
            preferred_element_type=F32,
        )
        start += rows
    out_ref[...] = total.astype(BF16)


def cut(down_ref, out_ref, *, start):
    out_ref[...] = down_ref[0, :, start : start + out_ref.shape[1]]


def products(total, where_ref, own_ref, far_ref, arrays, places, fresh):
    capacity = own_ref.shape[0]
    for array, first, count, mask in places:
        columns = pl.ds(pl.multiple_of(where_ref[mask] * count, min(count, 256)), count)
        block = arrays[array][first : first + count, :]
        for side, ref in enumerate((own_ref, far_ref)):
            lines = pl.ds(side * capacity, capacity)
            product = dot(ref[:, columns], block)
            if fresh:
                total[lines, :] = product
            else:
                total[lines, :] += product
        fresh = False


def first_units(where_ref, own_ref, far_ref, *refs, places):
    *arrays, total = refs
    products(total, where_ref, own_ref, far_ref, arrays, places, True)


def hidden_units(where_ref, own_ref, far_ref, start_ref, *refs, places, pairs):
    *arrays, out_ref, total = refs
    total[...] = start_ref[...]
    products(total, where_ref, own_ref, far_ref, arrays, places, False)
    half = total.shape[1] // 2
    if pairs == 0:
        gate, up = total[:, :half], total[:, half:]
        out_ref[...] = (gate / (1.0 + jnp.exp(-gate)) * up).astype(BF16)
        return
    block = half // (2 * pairs)
    device = where_ref[0]
    for y in range(2):
        for j in range(pairs):
            at = (2 * ((device // 4) ^ j) + ((device % 2) ^ y)) * block
            first = pl.ds(pl.multiple_of(at, 128), block)
            second = pl.ds(pl.multiple_of(half + at, 128), block)
            gate, up = total[:, first], total[:, second]
            at = (y * pairs + j) * block
            out_ref[:, at : at + block] = (gate / (1.0 + jnp.exp(-gate)) * up).astype(BF16)


def down_units(hidden_ref, *refs, places):
    arrays, (out_ref, away_ref) = refs[:-2], refs[-2:]
    capacity = out_ref.shape[0]
    total, unit = 0.0, 0
    for pieces in places:
        values = [arrays[a][r : r + n, c : c + w] for a, r, n, c, w in pieces]
        block = values[0] if len(values) == 1 else jnp.concatenate(values, axis=1)
        rows = block.shape[0]
        total = total + dot(hidden_ref[:, unit : unit + rows], block)
        unit += rows
    out_ref[...] = total[:capacity]
    away_ref[...] = total[capacity:].astype(BF16)


def weigh(place_ref, tag_ref, weights_ref, out_ref, away_ref, *sent_refs):
    total = out_ref[...] + away_ref[...].astype(F32)
    contribution = (weights_ref[...] * total).astype(BF16)
    step = total.shape[1]
    most, wide = sent_refs[0].shape
    for block, ref in enumerate(sent_refs):
        lines = pl.ds(block * most, most)
        ref[:, :step] = dot(place_ref[lines, :], contribution).astype(BF16)
        if wide > step:
            ref[:, step:] = tag_ref[lines, :]


def mix(*refs, step):
    returned, (select_ref, out_ref) = refs[:-2], refs[-2:]
    most, tok_dev = returned[0].shape[0], out_ref.shape[0]
    total = 0.0
    for block, ref in enumerate(returned):
        number = ref[:, step : step + 1].astype(jnp.int32) - 1
        table = (lax.broadcasted_iota(jnp.int32, (most, tok_dev), 1) == number).astype(BF16)
        select_ref[block * most : (block + 1) * most, :] = table
        total = total + lax.dot_general(
            table, ref[:, :step], (((0,), (0,)), ((), ())), preferred_element_type=F32
        )
    out_ref[...] = total.astype(BF16)


def mix_more(select_ref, *refs, ready):
    done, returned, out_ref = refs[:ready], refs[ready:-1], refs[-1]
    most = returned[0].shape[0]
    start = 0
    for ref in done:
        out_ref[:, start : start + ref.shape[1]] = ref[...]
        start += ref.shape[1]
    total = 0.0
    for block, ref in enumerate(returned):
        total = total + lax.dot_general(
            select_ref[block * most : (block + 1) * most, :],
            ref[...],
            (((0,), (0,)), ((), ())),
            preferred_element_type=F32,
        )
    out_ref[:, start:] = total.astype(BF16)


def per_device(tokens, choice_rows, gate_weights, w_gate, w_up, w_down):
    experts = lax.axis_size("expert")
    replicas = lax.axis_size("dp")
    expert = lax.axis_index("expert").astype(jnp.int32)
    replica = lax.axis_index("dp").astype(jnp.int32)
    tok_dev, width = tokens.shape
    most = tok_dev // 2
    own_rows = choice_rows[0]
    capacity = own_rows.shape[1]
    rows_shard, units = w_gate.shape[1:]
    block = units // replicas

    limit = 16 * 2**20 if capacity <= 128 else 48 * 2**20
    starts = [sum(SHARES[:i]) * width // sum(SHARES) for i in range(len(SHARES) + 1)]
    steps = [end - start for start, end in zip(starts, starts[1:])]
    down_rows = w_down.shape[1]
    pairs = replicas // 4
    zbit = replica // 2 % 2
    whole_lanes = block % 128 == 0
    if whole_lanes:
        def collect(flip, *arrays):
            count = sum(x.shape[1] * x.shape[2] for x in arrays[2:]) // units
            return pl.pallas_call(
                functools.partial(opening, flip=flip, pairs=pairs),
                out_shape=shape(rows_shard + count, units),
                in_specs=[pl.BlockSpec(memory_space=pltpu.SMEM)]
                + [pl.BlockSpec(memory_space=pl.ANY)] * len(arrays),
                out_specs=pl.BlockSpec(memory_space=pltpu.VMEM),
                scratch_shapes=[pltpu.SemaphoreType.DMA((2 * pairs + width // units,))],
                compiler_params=pltpu.CompilerParams(vmem_limit_bytes=OPENING_LIMIT),
                cost_estimate=pl.CostEstimate(flops=0, bytes_accessed=2**20, transcendentals=0),
            )(zbit[None], *arrays)

        other_units = collect(1, w_gate, w_up)
        across = collect(0, w_gate, w_up, w_down)
    else:
        same_units, other_units = (
            jnp.concatenate(
                [
                    lax.dynamic_index_in_dim(
                        w[0].reshape(rows_shard, pairs, 2, 2 * block), zbit ^ flip, axis=2, keepdims=False
                    ).reshape(rows_shard, units // 2)
                    for w in (w_gate, w_up)
                ],
                axis=1,
            )
            for flip in (0, 1)
        )
        halves = [w_down[0, :, at : at + units] for at in range(0, width, units)]
        across = jnp.concatenate([same_units, *halves], axis=0)
    far = [mask for mask in range(replicas - 2, 2, -2)]
    came = swap(across, "dp", 1)
    weights = {mask: swap(other_units, "dp", mask) for mask in far[::2]}


    def down_far(piece):
        own, bit = [piece], 4
        while bit < replicas:
            have = own[0] if len(own) == 1 else jnp.concatenate(own, axis=0)
            own.append(swap(have, "dp", bit))
            bit *= 2
        return own[1:]

    late_same, late_other = call(hand, [shape(rows_shard, units)] * 2, across, other_units)
    weights[2] = swap(late_other, "dp", 2)
    for mask in far[1::2]:
        weights[mask] = swap(late_same, "dp", mask)

    group = [tokens]
    bit = 1
    while bit < experts:
        have = group[0]
        if len(group) > 1:
            have = call(join, shape(bit * tok_dev, width), *group, wait=[other_units])
        group.append(swap(have, "expert", bit))
        bit *= 2
    piece = call(
        functools.partial(cut, start=0),
        shape(down_rows, steps[0]),
        w_down,
        wait=[weights[far[0]]],
        flops=LONG,
    )
    pick_hot, place_hot, tags = call(
        functools.partial(own_tables, experts=experts, tok_dev=tok_dev),
        [shape(experts * tok_dev, capacity), shape(experts * most, capacity), shape(experts * most, 128)],
        expert[None],
        own_rows,
        scalars=1,
    )
    picked = call(
        pick_rows,
        shape(capacity, width),
        pick_hot,
        *group,
        wait=[came, piece],
        flops=LONG,
    )
    picked_z = swap(picked, "dp", 2)
    group_far = [2, *far[::2]]
    came_far = [swap(weights[mask], "dp", 1) for mask in group_far]
    for mask in far[1::2]:
        weights[mask + 1] = swap(weights[mask], "dp", 1)

    down, down_far_y = [down_far(piece)], []
    for index in range(1, len(SHARES)):
        piece = call(
            functools.partial(cut, start=starts[index]),
            shape(down_rows, steps[index]),
            w_down,
            wait=[weights[far[-1]], piece],
        )
        down.append(down_far(piece))
    down_far_y.append([swap(x, "dp", 1) for x in down[0]])

    order = replica ^ jnp.arange(replicas, dtype=jnp.int32)
    late = [mask + 1 for mask in far[1::2]]
    arrays = [across, came, *came_far, *[weights[mask] for mask in group_far]]
    places = [(0, 0, rows_shard, 0), (1, 0, rows_shard, 1)]
    for i, mask in enumerate(group_far):
        places += [(2 + len(group_far) + i, 0, rows_shard, mask), (2 + i, 0, rows_shard, mask + 1)]
    for mask in far[1::2]:
        places.append((len(arrays), 0, rows_shard, mask))
        arrays.append(weights[mask])
    late_arrays = [weights[mask] for mask in late]
    late_places = [(i, 0, rows_shard, mask) for i, mask in enumerate(late)]
    if rows_shard % 128 != 0:
        blocks = {m: arrays[a][r : r + n] for a, r, n, m in places}
        blocks |= {m: late_arrays[a][r : r + n] for a, r, n, m in late_places}
        stacked = jnp.take(jnp.stack([blocks[m] for m in range(replicas)]), order, axis=0).reshape(-1, units)
        parts = stacked.shape[0] // 2
        arrays, late_arrays = [stacked[:parts]], [stacked[parts:]]
        places, late_places = [(0, 0, parts, 0)], [(0, 0, parts, 1)]
        order = jnp.arange(2, dtype=jnp.int32)
    flops = capacity * width * units
    start_units = call(
        functools.partial(first_units, places=places),
        shape(2 * capacity, units, dtype=F32),
        order,
        picked,
        picked_z,
        *arrays,
        flops=3 * flops,
        scalars=1,
    )
    hidden = pl.pallas_call(
        functools.partial(hidden_units, places=late_places, pairs=pairs if whole_lanes else 0),
        out_shape=shape(2 * capacity, units // 2),
        in_specs=[pl.BlockSpec(memory_space=pltpu.SMEM)]
        + [pl.BlockSpec(memory_space=pltpu.VMEM)] * (3 + len(late_arrays)),
        out_specs=pl.BlockSpec(memory_space=pltpu.VMEM),
        scratch_shapes=[pltpu.VMEM((2 * capacity, units), F32)],
        compiler_params=pltpu.CompilerParams(vmem_limit_bytes=limit),
        cost_estimate=pl.CostEstimate(flops=flops, bytes_accessed=2**22, transcendentals=0),
    )(order, picked, picked_z, start_units, *late_arrays)
    if not whole_lanes:
        index = jnp.arange(2 * pairs, dtype=jnp.int32)
        turn = 2 * ((replica // 4) ^ (index % pairs)) + ((replica % 2) ^ (index // pairs))
        hidden = jnp.take(hidden.reshape(-1, 2 * pairs, block), turn, axis=1).reshape(hidden.shape)

    gate_column = gate_weights[0, 0][:, None]
    results = []
    for index, (start, step, far_rows) in enumerate(zip(starts, steps, down)):
        if index > 0:
            held = call(hand, [shape(*x.shape) for x in far_rows], *far_rows, wait=[away])
            down_far_y.append([swap(x, "dp", 1) for x in held])

        def pieces(array, first, at, end):
            cuts = [(at, min(end, units)), (max(at, units), end)]
            return [
                (array, first + down_rows * (c // units), down_rows, c % units, e - c) for c, e in cuts if c < e
            ]

        parts = [across, came, *far_rows, *down_far_y[index]]
        count = len(far_rows)
        places = [pieces(0, rows_shard, start, start + step)]
        places += [[(2 + i, 0, x.shape[0], 0, step)] for i, x in enumerate(far_rows)]
        places += [pieces(1, rows_shard, start, start + step)]
        places += [[(2 + count + i, 0, x.shape[0], 0, step)] for i, x in enumerate(far_rows)]
        out, away = call(
            functools.partial(down_units, places=places),
            [shape(capacity, step, dtype=F32), shape(capacity, step)],
            hidden,
            *parts,
            wait=[away, sent[0]] if index else [],
            flops=LONG if index else 2 * capacity * units * step,
        )
        extra = 128 if index == 0 else 0
        sent = call(
            weigh,
            [shape(most, step + extra)] * experts,
            place_hot,
            tags,
            gate_column,
            out,
            swap(away, "dp", 2),
            flops=2 * experts * most * capacity * step,
        )
        returned = [sent[0]] + [swap(sent[c], "expert", c) for c in range(1, experts)]
        flops = 2 * experts * most * tok_dev * step
        if index == 0:
            select, result = call(
                functools.partial(mix, step=step),
                [shape(experts * most, tok_dev), shape(tok_dev, step)],
                *returned,
                flops=flops,
            )
            results.append(result)
        else:
            last = index == len(SHARES) - 1
            ready = results if last else []
            results.append(
                call(
                    functools.partial(mix_more, ready=len(ready)),
                    shape(tok_dev, width if last else step),
                    select,
                    *ready,
                    *returned,
                    flops=flops,
                )
            )
    return results[-1]


def solution(mesh):
    return jax.shard_map(
        per_device,
        mesh=mesh,
        in_specs=(
            P(("dp", "expert"), None),
            P("dp", "expert", None),
            P("dp", "expert", None),
            P("expert", "dp", None),
            P("expert", "dp", None),
            P("expert", "dp", None),
        ),
        out_specs=P(("dp", "expert"), None),
        check_vma=False,
    )
```

```python
import functools

import jax
import jax.numpy as jnp
from jax import lax
from jax.experimental import pallas as pl
from jax.experimental.pallas import tpu as pltpu
from jax.sharding import PartitionSpec as P

SHARES = (9, 7)
OPENING_LIMIT = 60 * 2**20
LONG = 10**12
F32 = jnp.float32
BF16 = jnp.bfloat16


def swap(value, axis, mask):
    pairs = [(source, source ^ mask) for source in range(lax.axis_size(axis))]
    return lax.ppermute(value, axis, pairs)


def call(kernel, out_shape, *args, wait=(), flops=0, scalars=0):
    args = (*args[:scalars], *wait, *args[scalars:])
    in_specs = [pl.BlockSpec(memory_space=pltpu.SMEM)] * scalars
    in_specs += [pl.BlockSpec(memory_space=pl.ANY)] * len(wait)
    in_specs += [pl.BlockSpec(memory_space=pltpu.VMEM)] * (len(args) - scalars - len(wait))
    outs = out_shape if isinstance(out_shape, (list, tuple)) else [out_shape]
    size = sum(a.size * a.dtype.itemsize for a in (*args, *outs))

    def body(*refs):
        kernel(*refs[:scalars], *refs[scalars + len(wait) :])

    return pl.pallas_call(
        body,
        out_shape=out_shape,
        in_specs=in_specs,
        out_specs=jax.tree.map(lambda _: pl.BlockSpec(memory_space=pltpu.VMEM), out_shape),
        compiler_params=pltpu.CompilerParams(vmem_limit_bytes=4 * size + 2**23),
        cost_estimate=pl.CostEstimate(flops=flops, bytes_accessed=size, transcendentals=0),
    )(*args)


def shape(*dims, dtype=BF16):
    return jax.ShapeDtypeStruct(dims, dtype)


def dot(a, b):
    return jnp.dot(a, b, preferred_element_type=F32)


def opening(bit_ref, gate_ref, up_ref, *refs, flip, pairs):
    *more, out_ref, sem = refs
    rows = gate_ref.shape[1]
    wide = gate_ref.shape[2] // (2 * pairs)
    copies = []

    def copy(source, target):
        copies.append(pltpu.make_async_copy(source, target, sem.at[len(copies)]))

    at = 0
    for ref in (gate_ref, up_ref):
        for j in range(pairs):
            start = pl.multiple_of((2 * j + (bit_ref[0] ^ flip)) * wide, 128)
            copy(ref.at[0, :, pl.ds(start, wide)], out_ref.at[:rows, at : at + wide])
            at += wide
    for down_ref in more:
        tall, half = down_ref.shape[1], out_ref.shape[1]
        for j in range(down_ref.shape[2] // half):
            copy(
                down_ref.at[0, :, j * half : (j + 1) * half],
                out_ref.at[rows + j * tall : rows + (j + 1) * tall],
            )
    for item in copies:
        item.start()
    for item in copies:
        item.wait()


def join(*refs):
    out_ref, start = refs[-1], 0
    for ref in refs[:-1]:
        out_ref[start : start + ref.shape[0]] = ref[...]
        start += ref.shape[0]


def hand(*refs):
    half = len(refs) // 2
    for ref, out_ref in zip(refs[:half], refs[half:]):
        out_ref[...] = ref[: out_ref.shape[0]]


def ranks_of(hits):
    c = hits.shape[1]
    before = lax.broadcasted_iota(jnp.int32, (c, c), 0) < lax.broadcasted_iota(jnp.int32, (c, c), 1)
    return dot(hits.astype(BF16), before.astype(BF16)).astype(jnp.int32)


def own_tables(expert_ref, rows_ref, pick_ref, place_ref, tag_ref, *, experts, tok_dev):
    rows = rows_ref[...]
    capacity = rows.shape[1]
    block = (rows // tok_dev) ^ expert_ref[0]
    local = rows % tok_dev
    place = block * tok_dev + local
    count = experts * tok_dev
    pick_ref[...] = (lax.broadcasted_iota(jnp.int32, (count, capacity), 0) == place).astype(BF16)
    hot = lax.broadcasted_iota(jnp.int32, (experts, capacity), 0) == block
    rank = jnp.sum(jnp.where(hot, ranks_of(hot.astype(F32)), 0), axis=0, keepdims=True)
    most = tok_dev // 2
    position = block * most + rank
    here = lax.broadcasted_iota(jnp.int32, (experts * most, capacity), 0) == position
    place_ref[...] = here.astype(BF16)
    number = jnp.sum(jnp.where(here, local + 1, 0).astype(F32), axis=1, keepdims=True)
    tag_ref[...] = jnp.broadcast_to(number, tag_ref.shape).astype(BF16)


def pick_rows(pick_ref, *refs):
    out_ref = refs[-1]
    total, start = 0.0, 0
    for ref in refs[:-1]:
        rows = ref.shape[0]
        total = total + lax.dot_general(
            pick_ref[start : start + rows, :],
            ref[...],
            (((0,), (0,)), ((), ())),
            preferred_element_type=F32,
        )
        start += rows
    out_ref[...] = total.astype(BF16)


def cut(down_ref, out_ref, *, start):
    out_ref[...] = down_ref[0, :, start : start + out_ref.shape[1]]


def products(total, where_ref, own_ref, far_ref, arrays, places, fresh):
    capacity = own_ref.shape[0]
    for array, first, count, mask in places:
        columns = pl.ds(pl.multiple_of(where_ref[mask] * count, min(count, 256)), count)
        block = arrays[array][first : first + count, :]
        for side, ref in enumerate((own_ref, far_ref)):
            lines = pl.ds(side * capacity, capacity)
            product = dot(ref[:, columns], block)
            if fresh:
                total[lines, :] = product
            else:
                total[lines, :] += product
        fresh = False


def first_units(where_ref, own_ref, far_ref, *refs, places):
    *arrays, total = refs
    products(total, where_ref, own_ref, far_ref, arrays, places, True)


def hidden_units(where_ref, own_ref, far_ref, start_ref, *refs, places, pairs):
    *arrays, out_ref, total = refs
    total[...] = start_ref[...]
    products(total, where_ref, own_ref, far_ref, arrays, places, False)
    half = total.shape[1] // 2
    if pairs == 0:
        gate, up = total[:, :half], total[:, half:]
        out_ref[...] = (gate / (1.0 + jnp.exp(-gate)) * up).astype(BF16)
        return
    block = half // (2 * pairs)
    device = where_ref[0]
    for y in range(2):
        for j in range(pairs):
            at = (2 * ((device // 4) ^ j) + ((device % 2) ^ y)) * block
            first = pl.ds(pl.multiple_of(at, 128), block)
            second = pl.ds(pl.multiple_of(half + at, 128), block)
            gate, up = total[:, first], total[:, second]
            at = (y * pairs + j) * block
            out_ref[:, at : at + block] = (gate / (1.0 + jnp.exp(-gate)) * up).astype(BF16)


def down_units(*refs, waits, counts, places):
    hidden_ref, refs = refs[waits], refs[waits + 1 :]
    far, near, (out_ref, away_ref, rows_ref, sem) = refs[: counts[0]], refs[counts[0] : -4], refs[-4:]
    capacity = out_ref.shape[0]
    copies, later = [], []
    for index, pieces in enumerate(places):
        at = 0
        for array, row, rows, column, columns in pieces:
            if array < counts[0]:
                copies.append(
                    pltpu.make_async_copy(
                        far[array].at[row : row + rows, column : column + columns],
                        rows_ref.at[array, :, at : at + columns],
                        sem.at[len(copies)],
                    )
                )
            at += columns
    for copy in copies:
        copy.start()
    total, unit = 0.0, 0
    for pieces in places:
        array, row, rows, column, columns = pieces[0]
        if array < counts[0]:
            later.append((unit, rows, array))
        else:
            block = near[array - counts[0]][row : row + rows, column : column + columns]
            total = total + dot(hidden_ref[:, unit : unit + rows], block)
        unit += rows
    for copy in copies:
        copy.wait()
    for unit, rows, array in later:
        total = total + dot(hidden_ref[:, unit : unit + rows], rows_ref[array])
    out_ref[...] = total[:capacity]
    away_ref[...] = total[capacity:].astype(BF16)


def weigh(place_ref, tag_ref, weights_ref, out_ref, away_ref, *sent_refs):
    total = out_ref[...] + away_ref[...].astype(F32)
    contribution = (weights_ref[...] * total).astype(BF16)
    step = total.shape[1]
    most, wide = sent_refs[0].shape
    for block, ref in enumerate(sent_refs):
        lines = pl.ds(block * most, most)
        ref[:, :step] = dot(place_ref[lines, :], contribution).astype(BF16)
        if wide > step:
            ref[:, step:] = tag_ref[lines, :]


def mix(*refs, step):
    returned, (select_ref, out_ref) = refs[:-2], refs[-2:]
    most, tok_dev = returned[0].shape[0], out_ref.shape[0]
    total = 0.0
    for block, ref in enumerate(returned):
        number = ref[:, step : step + 1].astype(jnp.int32) - 1
        table = (lax.broadcasted_iota(jnp.int32, (most, tok_dev), 1) == number).astype(BF16)
        select_ref[block * most : (block + 1) * most, :] = table
        total = total + lax.dot_general(
            table, ref[:, :step], (((0,), (0,)), ((), ())), preferred_element_type=F32
        )
    out_ref[...] = total.astype(BF16)


def mix_more(select_ref, *refs, ready):
    done, returned, out_ref = refs[:ready], refs[ready:-1], refs[-1]
    most = returned[0].shape[0]
    start = 0
    for ref in done:
        out_ref[:, start : start + ref.shape[1]] = ref[...]
        start += ref.shape[1]
    total = 0.0
    for block, ref in enumerate(returned):
        total = total + lax.dot_general(
            select_ref[block * most : (block + 1) * most, :],
            ref[...],
            (((0,), (0,)), ((), ())),
            preferred_element_type=F32,
        )
    out_ref[:, start:] = total.astype(BF16)


def per_device(tokens, choice_rows, gate_weights, w_gate, w_up, w_down):
    experts = lax.axis_size("expert")
    replicas = lax.axis_size("dp")
    expert = lax.axis_index("expert").astype(jnp.int32)
    replica = lax.axis_index("dp").astype(jnp.int32)
    tok_dev, width = tokens.shape
    most = tok_dev // 2
    own_rows = choice_rows[0]
    capacity = own_rows.shape[1]
    rows_shard, units = w_gate.shape[1:]
    block = units // replicas

    limit = 16 * 2**20 if capacity <= 128 else 48 * 2**20
    starts = [sum(SHARES[:i]) * width // sum(SHARES) for i in range(len(SHARES) + 1)]
    steps = [end - start for start, end in zip(starts, starts[1:])]
    down_rows = w_down.shape[1]
    pairs = replicas // 4
    zbit = replica // 2 % 2
    whole_lanes = block % 128 == 0
    if whole_lanes:
        def collect(flip, *arrays):
            count = sum(x.shape[1] * x.shape[2] for x in arrays[2:]) // units
            return pl.pallas_call(
                functools.partial(opening, flip=flip, pairs=pairs),
                out_shape=shape(rows_shard + count, units),
                in_specs=[pl.BlockSpec(memory_space=pltpu.SMEM)]
                + [pl.BlockSpec(memory_space=pl.ANY)] * len(arrays),
                out_specs=pl.BlockSpec(memory_space=pltpu.VMEM),
                scratch_shapes=[pltpu.SemaphoreType.DMA((2 * pairs + width // units,))],
                compiler_params=pltpu.CompilerParams(vmem_limit_bytes=OPENING_LIMIT),
                cost_estimate=pl.CostEstimate(flops=0, bytes_accessed=2**20, transcendentals=0),
            )(zbit[None], *arrays)

        other_units = collect(1, w_gate, w_up)
        across = collect(0, w_gate, w_up, w_down)
    else:
        same_units, other_units = (
            jnp.concatenate(
                [
                    lax.dynamic_index_in_dim(
                        w[0].reshape(rows_shard, pairs, 2, 2 * block), zbit ^ flip, axis=2, keepdims=False
                    ).reshape(rows_shard, units // 2)
                    for w in (w_gate, w_up)
                ],
                axis=1,
            )
            for flip in (0, 1)
        )
        halves = [w_down[0, :, at : at + units] for at in range(0, width, units)]
        across = jnp.concatenate([same_units, *halves], axis=0)
    far = [mask for mask in range(replicas - 2, 2, -2)]
    came = swap(across, "dp", 1)
    weights = {mask: swap(other_units, "dp", mask) for mask in far[::2]}


    def down_far(piece):
        own, bit = [piece], 4
        while bit < replicas:
            have = own[0] if len(own) == 1 else jnp.concatenate(own, axis=0)
            own.append(swap(have, "dp", bit))
            bit *= 2
        return own[1:]

    late_same, late_other = call(hand, [shape(rows_shard, units)] * 2, across, other_units)
    weights[2] = swap(late_other, "dp", 2)
    for mask in far[1::2]:
        weights[mask] = swap(late_same, "dp", mask)

    group = [tokens]
    bit = 1
    while bit < experts:
        have = group[0]
        if len(group) > 1:
            have = call(join, shape(bit * tok_dev, width), *group, wait=[other_units])
        group.append(swap(have, "expert", bit))
        bit *= 2
    piece = call(
        functools.partial(cut, start=0),
        shape(down_rows, steps[0]),
        w_down,
        wait=[weights[far[0]]],
        flops=LONG,
    )
    pick_hot, place_hot, tags = call(
        functools.partial(own_tables, experts=experts, tok_dev=tok_dev),
        [shape(experts * tok_dev, capacity), shape(experts * most, capacity), shape(experts * most, 128)],
        expert[None],
        own_rows,
        scalars=1,
    )
    picked = call(
        pick_rows,
        shape(capacity, width),
        pick_hot,
        *group,
        wait=[came, piece],
        flops=LONG,
    )
    picked_z = swap(picked, "dp", 2)
    group_far = [2, *far[::2]]
    came_far = [swap(weights[mask], "dp", 1) for mask in group_far]
    for mask in far[1::2]:
        weights[mask + 1] = swap(weights[mask], "dp", 1)

    down, down_far_y = [down_far(piece)], []
    for index in range(1, len(SHARES)):
        piece = call(
            functools.partial(cut, start=starts[index]),
            shape(down_rows, steps[index]),
            w_down,
            wait=[weights[far[-1]], piece],
        )
        down.append(down_far(piece))
    down_far_y.append([swap(x, "dp", 1) for x in down[0]])

    order = replica ^ jnp.arange(replicas, dtype=jnp.int32)
    late = [mask + 1 for mask in far[1::2]]
    arrays = [across, came, *came_far, *[weights[mask] for mask in group_far]]
    places = [(0, 0, rows_shard, 0), (1, 0, rows_shard, 1)]
    for i, mask in enumerate(group_far):
        places += [(2 + len(group_far) + i, 0, rows_shard, mask), (2 + i, 0, rows_shard, mask + 1)]
    for mask in far[1::2]:
        places.append((len(arrays), 0, rows_shard, mask))
        arrays.append(weights[mask])
    late_arrays = [weights[mask] for mask in late]
    late_places = [(i, 0, rows_shard, mask) for i, mask in enumerate(late)]
    if rows_shard % 128 != 0:
        blocks = {m: arrays[a][r : r + n] for a, r, n, m in places}
        blocks |= {m: late_arrays[a][r : r + n] for a, r, n, m in late_places}
        stacked = jnp.take(jnp.stack([blocks[m] for m in range(replicas)]), order, axis=0).reshape(-1, units)
        parts = stacked.shape[0] // 2
        arrays, late_arrays = [stacked[:parts]], [stacked[parts:]]
        places, late_places = [(0, 0, parts, 0)], [(0, 0, parts, 1)]
        order = jnp.arange(2, dtype=jnp.int32)
    flops = capacity * width * units
    start_units = call(
        functools.partial(first_units, places=places),
        shape(2 * capacity, units, dtype=F32),
        order,
        picked,
        picked_z,
        *arrays,
        flops=3 * flops,
        scalars=1,
    )
    hidden = pl.pallas_call(
        functools.partial(hidden_units, places=late_places, pairs=pairs if whole_lanes else 0),
        out_shape=shape(2 * capacity, units // 2),
        in_specs=[pl.BlockSpec(memory_space=pltpu.SMEM)]
        + [pl.BlockSpec(memory_space=pltpu.VMEM)] * (3 + len(late_arrays)),
        out_specs=pl.BlockSpec(memory_space=pltpu.VMEM),
        scratch_shapes=[pltpu.VMEM((2 * capacity, units), F32)],
        compiler_params=pltpu.CompilerParams(vmem_limit_bytes=limit),
        cost_estimate=pl.CostEstimate(flops=flops, bytes_accessed=2**22, transcendentals=0),
    )(order, picked, picked_z, start_units, *late_arrays)
    if not whole_lanes:
        index = jnp.arange(2 * pairs, dtype=jnp.int32)
        turn = 2 * ((replica // 4) ^ (index % pairs)) + ((replica % 2) ^ (index // pairs))
        hidden = jnp.take(hidden.reshape(-1, 2 * pairs, block), turn, axis=1).reshape(hidden.shape)

    gate_column = gate_weights[0, 0][:, None]
    results = []
    for index, (start, step, far_rows) in enumerate(zip(starts, steps, down)):
        if index > 0:
            held = call(hand, [shape(*x.shape) for x in far_rows], *far_rows, wait=[away])
            down_far_y.append([swap(x, "dp", 1) for x in held])

        def pieces(array, first, at, end):
            cuts = [(at, min(end, units)), (max(at, units), end)]
            return [
                (array, first + down_rows * (c // units), down_rows, c % units, e - c) for c, e in cuts if c < e
            ]

        parts = [across, came, *far_rows, *down_far_y[index]]
        count = len(far_rows)
        places = [pieces(0, rows_shard, start, start + step)]
        places += [[(2 + i, 0, x.shape[0], 0, step)] for i, x in enumerate(far_rows)]
        places += [pieces(1, rows_shard, start, start + step)]
        places += [[(2 + count + i, 0, x.shape[0], 0, step)] for i, x in enumerate(far_rows)]
        waits = [away, sent[0]] if index else []
        out, away = pl.pallas_call(
            functools.partial(down_units, waits=len(waits), counts=(2, len(parts) - 2), places=places),
            out_shape=[shape(capacity, step, dtype=F32), shape(capacity, step)],
            in_specs=[pl.BlockSpec(memory_space=pl.ANY)] * len(waits)
            + [pl.BlockSpec(memory_space=pltpu.VMEM)]
            + [pl.BlockSpec(memory_space=pl.ANY)] * 2
            + [pl.BlockSpec(memory_space=pltpu.VMEM)] * (len(parts) - 2),
            out_specs=[pl.BlockSpec(memory_space=pltpu.VMEM)] * 2,
            scratch_shapes=[
                pltpu.VMEM((2, down_rows, step), BF16),
                pltpu.SemaphoreType.DMA((2 * (width // units),)),
            ],
            compiler_params=pltpu.CompilerParams(vmem_limit_bytes=limit),
            cost_estimate=pl.CostEstimate(
                flops=LONG if index else 2 * capacity * units * step,
                bytes_accessed=2**22,
                transcendentals=0,
            ),
        )(*waits, hidden, *parts)
        extra = 128 if index == 0 else 0
        sent = call(
            weigh,
            [shape(most, step + extra)] * experts,
            place_hot,
            tags,
            gate_column,
            out,
            swap(away, "dp", 2),
            flops=2 * experts * most * capacity * step,
        )
        returned = [sent[0]] + [swap(sent[c], "expert", c) for c in range(1, experts)]
        flops = 2 * experts * most * tok_dev * step
        if index == 0:
            select, result = call(
                functools.partial(mix, step=step),
                [shape(experts * most, tok_dev), shape(tok_dev, step)],
                *returned,
                flops=flops,
            )
            results.append(result)
        else:
            last = index == len(SHARES) - 1
            ready = results if last else []
            results.append(
                call(
                    functools.partial(mix_more, ready=len(ready)),
                    shape(tok_dev, width if last else step),
                    select,
                    *ready,
                    *returned,
                    flops=flops,
                )
            )
    return results[-1]


def solution(mesh):
    return jax.shard_map(
        per_device,
        mesh=mesh,
        in_specs=(
            P(("dp", "expert"), None),
            P("dp", "expert", None),
            P("dp", "expert", None),
            P("expert", "dp", None),
            P("expert", "dp", None),
            P("expert", "dp", None),
        ),
        out_specs=P(("dp", "expert"), None),
        check_vma=False,
    )
```

```python
import functools

import jax
import jax.numpy as jnp
from jax import lax
from jax.experimental import pallas as pl
from jax.experimental.pallas import tpu as pltpu
from jax.sharding import PartitionSpec as P

SHARES = (9, 7)
OPENING_LIMIT = 60 * 2**20
LONG = 10**12
F32 = jnp.float32
BF16 = jnp.bfloat16


def swap(value, axis, mask):
    pairs = [(source, source ^ mask) for source in range(lax.axis_size(axis))]
    return lax.ppermute(value, axis, pairs)


def call(kernel, out_shape, *args, wait=(), flops=0, scalars=0):
    args = (*args[:scalars], *wait, *args[scalars:])
    in_specs = [pl.BlockSpec(memory_space=pltpu.SMEM)] * scalars
    in_specs += [pl.BlockSpec(memory_space=pl.ANY)] * len(wait)
    in_specs += [pl.BlockSpec(memory_space=pltpu.VMEM)] * (len(args) - scalars - len(wait))
    outs = out_shape if isinstance(out_shape, (list, tuple)) else [out_shape]
    size = sum(a.size * a.dtype.itemsize for a in (*args, *outs))

    def body(*refs):
        kernel(*refs[:scalars], *refs[scalars + len(wait) :])

    return pl.pallas_call(
        body,
        out_shape=out_shape,
        in_specs=in_specs,
        out_specs=jax.tree.map(lambda _: pl.BlockSpec(memory_space=pltpu.VMEM), out_shape),
        compiler_params=pltpu.CompilerParams(vmem_limit_bytes=4 * size + 2**23),
        cost_estimate=pl.CostEstimate(flops=flops, bytes_accessed=size, transcendentals=0),
    )(*args)


def shape(*dims, dtype=BF16):
    return jax.ShapeDtypeStruct(dims, dtype)


def dot(a, b):
    return jnp.dot(a, b, preferred_element_type=F32)


def opening(bit_ref, gate_ref, up_ref, *refs, flip, pairs):
    *more, out_ref, sem = refs
    rows = gate_ref.shape[1]
    wide = gate_ref.shape[2] // (2 * pairs)
    copies = []

    def copy(source, target):
        copies.append(pltpu.make_async_copy(source, target, sem.at[len(copies)]))

    at = 0
    for ref in (gate_ref, up_ref):
        for j in range(pairs):
            start = pl.multiple_of((2 * j + (bit_ref[0] ^ flip)) * wide, 128)
            copy(ref.at[0, :, pl.ds(start, wide)], out_ref.at[:rows, at : at + wide])
            at += wide
    for down_ref in more:
        tall, half = down_ref.shape[1], out_ref.shape[1]
        for j in range(down_ref.shape[2] // half):
            copy(
                down_ref.at[0, :, j * half : (j + 1) * half],
                out_ref.at[rows + j * tall : rows + (j + 1) * tall],
            )
    for item in copies:
        item.start()
    for item in copies:
        item.wait()


def join(*refs):
    out_ref, start = refs[-1], 0
    for ref in refs[:-1]:
        out_ref[start : start + ref.shape[0]] = ref[...]
        start += ref.shape[0]


def hand(*refs):
    half = len(refs) // 2
    for ref, out_ref in zip(refs[:half], refs[half:]):
        out_ref[...] = ref[: out_ref.shape[0]]


def ranks_of(hits):
    c = hits.shape[1]
    before = lax.broadcasted_iota(jnp.int32, (c, c), 0) < lax.broadcasted_iota(jnp.int32, (c, c), 1)
    return dot(hits.astype(BF16), before.astype(BF16)).astype(jnp.int32)


def own_tables(expert_ref, rows_ref, pick_ref, place_ref, tag_ref, *, experts, tok_dev):
    rows = rows_ref[...]
    capacity = rows.shape[1]
    block = (rows // tok_dev) ^ expert_ref[0]
    local = rows % tok_dev
    place = block * tok_dev + local
    count = experts * tok_dev
    pick_ref[...] = (lax.broadcasted_iota(jnp.int32, (count, capacity), 0) == place).astype(BF16)
    hot = lax.broadcasted_iota(jnp.int32, (experts, capacity), 0) == block
    rank = jnp.sum(jnp.where(hot, ranks_of(hot.astype(F32)), 0), axis=0, keepdims=True)
    most = tok_dev // 2
    position = block * most + rank
    here = lax.broadcasted_iota(jnp.int32, (experts * most, capacity), 0) == position
    place_ref[...] = here.astype(BF16)
    number = jnp.sum(jnp.where(here, local + 1, 0).astype(F32), axis=1, keepdims=True)
    tag_ref[...] = jnp.broadcast_to(number, tag_ref.shape).astype(BF16)


def pick_rows(pick_ref, *refs):
    out_ref = refs[-1]
    total, start = 0.0, 0
    for ref in refs[:-1]:
        rows = ref.shape[0]
        total = total + lax.dot_general(
            pick_ref[start : start + rows, :],
            ref[...],
            (((0,), (0,)), ((), ())),
            preferred_element_type=F32,
        )
        start += rows
    out_ref[...] = total.astype(BF16)


def cut(down_ref, out_ref, *, start):
    out_ref[...] = down_ref[0, :, start : start + out_ref.shape[1]]


def products(total, where_ref, own_ref, far_ref, arrays, places, fresh):
    capacity = own_ref.shape[0]
    for array, first, count, mask in places:
        columns = pl.ds(pl.multiple_of(where_ref[mask] * count, min(count, 256)), count)
        block = arrays[array][first : first + count, :]
        for side, ref in enumerate((own_ref, far_ref)):
            lines = pl.ds(side * capacity, capacity)
            product = dot(ref[:, columns], block)
            if fresh:
                total[lines, :] = product
            else:
                total[lines, :] += product
        fresh = False


def first_units(where_ref, own_ref, far_ref, *refs, places):
    *arrays, total = refs
    products(total, where_ref, own_ref, far_ref, arrays, places, True)


def hidden_units(where_ref, own_ref, far_ref, start_ref, *refs, places, pairs):
    *arrays, out_ref, total = refs
    total[...] = start_ref[...]
    products(total, where_ref, own_ref, far_ref, arrays, places, False)
    half = total.shape[1] // 2
    if pairs == 0:
        gate, up = total[:, :half], total[:, half:]
        out_ref[...] = (gate / (1.0 + jnp.exp(-gate)) * up).astype(BF16)
        return
    block = half // (2 * pairs)
    device = where_ref[0]
    for y in range(2):
        for j in range(pairs):
            at = (2 * ((device // 4) ^ j) + ((device % 2) ^ y)) * block
            first = pl.ds(pl.multiple_of(at, 128), block)
            second = pl.ds(pl.multiple_of(half + at, 128), block)
            gate, up = total[:, first], total[:, second]
            at = (y * pairs + j) * block
            out_ref[:, at : at + block] = (gate / (1.0 + jnp.exp(-gate)) * up).astype(BF16)


def down_units(*refs, waits, counts, places, side):
    hidden_ref, refs = refs[waits], refs[waits + 1 :]
    far, near, (out_ref, rows_ref, sem) = refs[: counts[0]], refs[counts[0] : -3], refs[-3:]
    lines = pl.ds(side * out_ref.shape[0], out_ref.shape[0])
    copies, later = [], []
    for index, pieces in enumerate(places):
        at = 0
        for array, row, rows, column, columns in pieces:
            if array < counts[0]:
                copies.append(
                    pltpu.make_async_copy(
                        far[array].at[row : row + rows, column : column + columns],
                        rows_ref.at[array, :, at : at + columns],
                        sem.at[len(copies)],
                    )
                )
            at += columns
    for copy in copies:
        copy.start()
    total, unit = 0.0, 0
    for pieces in places:
        array, row, rows, column, columns = pieces[0]
        if array < counts[0]:
            later.append((unit, rows, array))
        else:
            block = near[array - counts[0]][row : row + rows, column : column + columns]
            total = total + dot(hidden_ref[lines, unit : unit + rows], block)
        unit += rows
    for copy in copies:
        copy.wait()
    for unit, rows, array in later:
        total = total + dot(hidden_ref[lines, unit : unit + rows], rows_ref[array])
    out_ref[...] = total.astype(out_ref.dtype)


def weigh(place_ref, tag_ref, weights_ref, out_ref, away_ref, *sent_refs):
    total = out_ref[...] + away_ref[...].astype(F32)
    contribution = (weights_ref[...] * total).astype(BF16)
    step = total.shape[1]
    most, wide = sent_refs[0].shape
    for block, ref in enumerate(sent_refs):
        lines = pl.ds(block * most, most)
        ref[:, :step] = dot(place_ref[lines, :], contribution).astype(BF16)
        if wide > step:
            ref[:, step:] = tag_ref[lines, :]


def mix(*refs, step):
    returned, (select_ref, out_ref) = refs[:-2], refs[-2:]
    most, tok_dev = returned[0].shape[0], out_ref.shape[0]
    total = 0.0
    for block, ref in enumerate(returned):
        number = ref[:, step : step + 1].astype(jnp.int32) - 1
        table = (lax.broadcasted_iota(jnp.int32, (most, tok_dev), 1) == number).astype(BF16)
        select_ref[block * most : (block + 1) * most, :] = table
        total = total + lax.dot_general(
            table, ref[:, :step], (((0,), (0,)), ((), ())), preferred_element_type=F32
        )
    out_ref[...] = total.astype(BF16)


def mix_more(select_ref, *refs, ready):
    done, returned, out_ref = refs[:ready], refs[ready:-1], refs[-1]
    most = returned[0].shape[0]
    start = 0
    for ref in done:
        out_ref[:, start : start + ref.shape[1]] = ref[...]
        start += ref.shape[1]
    total = 0.0
    for block, ref in enumerate(returned):
        total = total + lax.dot_general(
            select_ref[block * most : (block + 1) * most, :],
            ref[...],
            (((0,), (0,)), ((), ())),
            preferred_element_type=F32,
        )
    out_ref[:, start:] = total.astype(BF16)


def per_device(tokens, choice_rows, gate_weights, w_gate, w_up, w_down):
    experts = lax.axis_size("expert")
    replicas = lax.axis_size("dp")
    expert = lax.axis_index("expert").astype(jnp.int32)
    replica = lax.axis_index("dp").astype(jnp.int32)
    tok_dev, width = tokens.shape
    most = tok_dev // 2
    own_rows = choice_rows[0]
    capacity = own_rows.shape[1]
    rows_shard, units = w_gate.shape[1:]
    block = units // replicas

    limit = 16 * 2**20 if capacity <= 128 else 48 * 2**20
    starts = [sum(SHARES[:i]) * width // sum(SHARES) for i in range(len(SHARES) + 1)]
    steps = [end - start for start, end in zip(starts, starts[1:])]
    down_rows = w_down.shape[1]
    pairs = replicas // 4
    zbit = replica // 2 % 2
    whole_lanes = block % 128 == 0
    if whole_lanes:
        def collect(flip, *arrays):
            count = sum(x.shape[1] * x.shape[2] for x in arrays[2:]) // units
            return pl.pallas_call(
                functools.partial(opening, flip=flip, pairs=pairs),
                out_shape=shape(rows_shard + count, units),
                in_specs=[pl.BlockSpec(memory_space=pltpu.SMEM)]
                + [pl.BlockSpec(memory_space=pl.ANY)] * len(arrays),
                out_specs=pl.BlockSpec(memory_space=pltpu.VMEM),
                scratch_shapes=[pltpu.SemaphoreType.DMA((2 * pairs + width // units,))],
                compiler_params=pltpu.CompilerParams(vmem_limit_bytes=OPENING_LIMIT),
                cost_estimate=pl.CostEstimate(flops=0, bytes_accessed=2**20, transcendentals=0),
            )(zbit[None], *arrays)

        other_units = collect(1, w_gate, w_up)
        across = collect(0, w_gate, w_up, w_down)
    else:
        same_units, other_units = (
            jnp.concatenate(
                [
                    lax.dynamic_index_in_dim(
                        w[0].reshape(rows_shard, pairs, 2, 2 * block), zbit ^ flip, axis=2, keepdims=False
                    ).reshape(rows_shard, units // 2)
                    for w in (w_gate, w_up)
                ],
                axis=1,
            )
            for flip in (0, 1)
        )
        halves = [w_down[0, :, at : at + units] for at in range(0, width, units)]
        across = jnp.concatenate([same_units, *halves], axis=0)
    far = [mask for mask in range(replicas - 2, 2, -2)]
    came = swap(across, "dp", 1)
    weights = {mask: swap(other_units, "dp", mask) for mask in far[::2]}


    def down_far(piece):
        own, bit = [piece], 4
        while bit < replicas:
            have = own[0] if len(own) == 1 else jnp.concatenate(own, axis=0)
            own.append(swap(have, "dp", bit))
            bit *= 2
        return own[1:]

    late_same, late_other = call(hand, [shape(rows_shard, units)] * 2, across, other_units)
    weights[2] = swap(late_other, "dp", 2)
    for mask in far[1::2]:
        weights[mask] = swap(late_same, "dp", mask)

    group = [tokens]
    bit = 1
    while bit < experts:
        have = group[0]
        if len(group) > 1:
            have = call(join, shape(bit * tok_dev, width), *group, wait=[other_units])
        group.append(swap(have, "expert", bit))
        bit *= 2
    piece = call(
        functools.partial(cut, start=0),
        shape(down_rows, steps[0]),
        w_down,
        wait=[weights[far[0]]],
        flops=LONG,
    )
    pick_hot, place_hot, tags = call(
        functools.partial(own_tables, experts=experts, tok_dev=tok_dev),
        [shape(experts * tok_dev, capacity), shape(experts * most, capacity), shape(experts * most, 128)],
        expert[None],
        own_rows,
        scalars=1,
    )
    picked = call(
        pick_rows,
        shape(capacity, width),
        pick_hot,
        *group,
        wait=[came, piece],
        flops=LONG,
    )
    picked_z = swap(picked, "dp", 2)
    group_far = [2, *far[::2]]
    came_far = [swap(weights[mask], "dp", 1) for mask in group_far]
    for mask in far[1::2]:
        weights[mask + 1] = swap(weights[mask], "dp", 1)

    down, down_far_y = [down_far(piece)], []
    for index in range(1, len(SHARES)):
        piece = call(
            functools.partial(cut, start=starts[index]),
            shape(down_rows, steps[index]),
            w_down,
            wait=[weights[far[-1]], piece],
        )
        down.append(down_far(piece))
    down_far_y.append([swap(x, "dp", 1) for x in down[0]])

    order = replica ^ jnp.arange(replicas, dtype=jnp.int32)
    late = [mask + 1 for mask in far[1::2]]
    arrays = [across, came, *came_far, *[weights[mask] for mask in group_far]]
    places = [(0, 0, rows_shard, 0), (1, 0, rows_shard, 1)]
    for i, mask in enumerate(group_far):
        places += [(2 + len(group_far) + i, 0, rows_shard, mask), (2 + i, 0, rows_shard, mask + 1)]
    for mask in far[1::2]:
        places.append((len(arrays), 0, rows_shard, mask))
        arrays.append(weights[mask])
    late_arrays = [weights[mask] for mask in late]
    late_places = [(i, 0, rows_shard, mask) for i, mask in enumerate(late)]
    if rows_shard % 128 != 0:
        blocks = {m: arrays[a][r : r + n] for a, r, n, m in places}
        blocks |= {m: late_arrays[a][r : r + n] for a, r, n, m in late_places}
        stacked = jnp.take(jnp.stack([blocks[m] for m in range(replicas)]), order, axis=0).reshape(-1, units)
        parts = stacked.shape[0] // 2
        arrays, late_arrays = [stacked[:parts]], [stacked[parts:]]
        places, late_places = [(0, 0, parts, 0)], [(0, 0, parts, 1)]
        order = jnp.arange(2, dtype=jnp.int32)
    flops = capacity * width * units
    start_units = call(
        functools.partial(first_units, places=places),
        shape(2 * capacity, units, dtype=F32),
        order,
        picked,
        picked_z,
        *arrays,
        flops=3 * flops,
        scalars=1,
    )
    hidden = pl.pallas_call(
        functools.partial(hidden_units, places=late_places, pairs=pairs if whole_lanes else 0),
        out_shape=shape(2 * capacity, units // 2),
        in_specs=[pl.BlockSpec(memory_space=pltpu.SMEM)]
        + [pl.BlockSpec(memory_space=pltpu.VMEM)] * (3 + len(late_arrays)),
        out_specs=pl.BlockSpec(memory_space=pltpu.VMEM),
        scratch_shapes=[pltpu.VMEM((2 * capacity, units), F32)],
        compiler_params=pltpu.CompilerParams(vmem_limit_bytes=limit),
        cost_estimate=pl.CostEstimate(flops=flops, bytes_accessed=2**22, transcendentals=0),
    )(order, picked, picked_z, start_units, *late_arrays)
    if not whole_lanes:
        index = jnp.arange(2 * pairs, dtype=jnp.int32)
        turn = 2 * ((replica // 4) ^ (index % pairs)) + ((replica % 2) ^ (index // pairs))
        hidden = jnp.take(hidden.reshape(-1, 2 * pairs, block), turn, axis=1).reshape(hidden.shape)

    gate_column = gate_weights[0, 0][:, None]
    results = []
    for index, (start, step, far_rows) in enumerate(zip(starts, steps, down)):
        if index > 0:
            held = call(hand, [shape(*x.shape) for x in far_rows], *far_rows, wait=[away])
            down_far_y.append([swap(x, "dp", 1) for x in held])

        def pieces(array, first, at, end):
            cuts = [(at, min(end, units)), (max(at, units), end)]
            return [
                (array, first + down_rows * (c // units), down_rows, c % units, e - c) for c, e in cuts if c < e
            ]

        parts = [across, came, *far_rows, *down_far_y[index]]
        count = len(far_rows)
        places = [pieces(0, rows_shard, start, start + step)]
        places += [[(2 + i, 0, x.shape[0], 0, step)] for i, x in enumerate(far_rows)]
        places += [pieces(1, rows_shard, start, start + step)]
        places += [[(2 + count + i, 0, x.shape[0], 0, step)] for i, x in enumerate(far_rows)]
        waits = [away, sent[0]] if index else []
        halves = []
        for side, dtype in ((1, BF16), (0, F32)):
            halves.append(
                pl.pallas_call(
                    functools.partial(
                        down_units, waits=len(waits), counts=(2, len(parts) - 2), places=places, side=side
                    ),
                    out_shape=shape(capacity, step, dtype=dtype),
                    in_specs=[pl.BlockSpec(memory_space=pl.ANY)] * len(waits)
                    + [pl.BlockSpec(memory_space=pltpu.VMEM)]
                    + [pl.BlockSpec(memory_space=pl.ANY)] * 2
                    + [pl.BlockSpec(memory_space=pltpu.VMEM)] * (len(parts) - 2),
                    out_specs=pl.BlockSpec(memory_space=pltpu.VMEM),
                    scratch_shapes=[
                        pltpu.VMEM((2, down_rows, step), BF16),
                        pltpu.SemaphoreType.DMA((2 * (width // units),)),
                    ],
                    compiler_params=pltpu.CompilerParams(vmem_limit_bytes=limit),
                    cost_estimate=pl.CostEstimate(
                        flops=LONG if index and side else capacity * units * step,
                        bytes_accessed=2**22,
                        transcendentals=0,
                    ),
                )(*waits, hidden, *parts)
            )
            waits = halves[:1]
        away, out = halves
        extra = 128 if index == 0 else 0
        sent = call(
            weigh,
            [shape(most, step + extra)] * experts,
            place_hot,
            tags,
            gate_column,
            out,
            swap(away, "dp", 2),
            flops=2 * experts * most * capacity * step,
        )
        returned = [sent[0]] + [swap(sent[c], "expert", c) for c in range(1, experts)]
        flops = 2 * experts * most * tok_dev * step
        if index == 0:
            select, result = call(
                functools.partial(mix, step=step),
                [shape(experts * most, tok_dev), shape(tok_dev, step)],
                *returned,
                flops=flops,
            )
            results.append(result)
        else:
            last = index == len(SHARES) - 1
            ready = results if last else []
            results.append(
                call(
                    functools.partial(mix_more, ready=len(ready)),
                    shape(tok_dev, width if last else step),
                    select,
                    *ready,
                    *returned,
                    flops=flops,
                )
            )
    return results[-1]


def solution(mesh):
    return jax.shard_map(
        per_device,
        mesh=mesh,
        in_specs=(
            P(("dp", "expert"), None),
            P("dp", "expert", None),
            P("dp", "expert", None),
            P("expert", "dp", None),
            P("expert", "dp", None),
            P("expert", "dp", None),
        ),
        out_specs=P(("dp", "expert"), None),
        check_vma=False,
    )
```
